512 devices in a mesh: seq: 32 (over z, x_hi), tp: 16 (over y, x_lo, core).
Axes of the slice: x: 4 (x_hi: 2, x_lo: 2; x = x_hi * 2 + x_lo), y: 4, z: 16, core: 2. Of those that a mesh axis runs over, the one named last changes fastest.
Arguments:
- stream_q: bfloat16 [4096, 16384], P('tp', 'seq'), may hold values from -6 to 6
- stream_k: bfloat16 [4096, 16384], P('tp', 'seq'), may hold values from -6 to 6
- stream_v: bfloat16 [4096, 16384], P('tp', 'seq'), may hold values from -6 to 6
- short_taps: float32 [3, 4096, 3], P(None, 'tp'), may hold values from -3 to 3
- filters: float32 [256, 16384], P('tp', 'seq'), may hold values from -2.5 to 2.5
- live_mask: int32 [4096], P('tp'), may hold values from 0 to 1, as said below
- skip_gain: float32 [4096], P('tp'), may hold values from 0.5 to 1.5
Outputs:
- gated_out: bfloat16 [4096, 16384], P('tp', 'seq')
The draws below stay inside these ranges and needn't reach their ends.
Inputs may be any that keep to these rules, and one draw needn't show every extreme that they name: `live_mask`: in each block of 256 channels the dummy channels, if any, form the block's tail.
All inputs are finite; a program needn't handle non-finite values.
Results may differ from the reference program's by a relative error of at most 0.0054.
Values may be sent and summed in bfloat16 or wider, within the bound.
No kernel may reach another device: no remote copies, remote signals or barrier semaphores. Data moves between devices by JAX's collectives and lax.ppermute only.
A program may use at most 64 MiB of HBM per device.

```python
import jax
import jax.numpy as jnp
from jax import lax

C = 4096
G = 256
L = 16384
CH_TP = 256


def draw_filters(key, part):
    key = jax.random.fold_in(key, 11)
    pick_key, fast_key, slow_key, gain_key, rough_key = jax.random.split(key, 5)
    fast_share = 0.5
    chooser = jax.random.uniform(pick_key, (G, 1), jnp.float32)
    scale_fast = jax.random.uniform(fast_key, (G, 1), jnp.float32, 30.0, 50.0)
    scale_slow = jax.random.uniform(slow_key, (G, 1), jnp.float32, 0.5, 4.0) * L
    time_scale = jnp.where(chooser < fast_share, scale_fast, scale_slow)
    positions = jnp.arange(L, dtype=jnp.float32)[None, :]
    envelope = jnp.exp(-positions / time_scale)
    energy = jnp.expm1(-2.0 * L / time_scale) / jnp.expm1(-2.0 / time_scale)
    group_gain = jnp.exp(jax.random.uniform(gain_key, (G, 1), jnp.float32, -0.7, 0.7))
    rough_part = jnp.clip(jax.random.normal(rough_key, (G, L), jnp.float32), -4.0, 4.0)
    return group_gain * envelope * rough_part / jnp.sqrt(energy)


def draw_live_mask(key, part):
    key = jax.random.fold_in(key, 23)
    block_total = C // CH_TP
    dummies = jax.random.randint(key, (block_total, 1), 0, CH_TP // 4 + 1)
    position = jnp.arange(CH_TP, dtype=jnp.int32)[None, :]
    return (position < CH_TP - dummies).astype(jnp.int32).reshape(C)


def level_of(own_key, shape, cuts, least, largest):
    gain, own = 1.0, jax.random.fold_in(own_key, 6)
    for axis_at, blocks in cuts:
        heights = jnp.exp(jax.random.uniform(jax.random.fold_in(own, axis_at), (blocks,), jnp.float32, least / len(cuts), largest / len(cuts)))
        gain = gain * jnp.repeat(heights, shape[axis_at] // blocks).reshape([-1 if axis == axis_at else 1 for axis in range(len(shape))])
    return gain


def bell_draw(stream_key, shape, deviation, limit, cuts=(), kind=jnp.bfloat16):
    factor_of = level_of(stream_key, shape, cuts, -0.22, 0.18) if cuts else 1.0
    values = jax.random.normal(stream_key, shape, jnp.float32) * deviation * factor_of
    return jnp.minimum(jnp.maximum(values, -limit), limit).astype(kind)


def setup_inputs(seed: int = 0) -> dict:
    key_list = jax.random.split(jax.random.key(seed), 8)
    stream_q = bell_draw(key_list[0], (C, L), 1.0, 6.0, ((0, 16), (1, 32)))
    stream_k = bell_draw(key_list[1], (C, L), 1.0, 6.0, ((0, 16), (1, 32)))
    stream_v = bell_draw(key_list[2], (C, L), 1.0, 6.0, ((0, 16), (1, 32)))
    short_taps = bell_draw(key_list[3], (3, C, 3), 0.6, 3.0, ((1, 16),), jnp.float32)
    filters = draw_filters(jax.random.fold_in(key_list[7], 71), 0)
    live_mask = draw_live_mask(jax.random.fold_in(key_list[7], 71), 0)
    skip_gain = jnp.clip(0.5 + 1.0 * jax.random.uniform(key_list[6], (C,), jnp.float32) ** level_of(key_list[6], (C,), ((0, 16),), -0.2, 0.2), 0.5, 1.5)
    return {"stream_q": stream_q, "stream_k": stream_k, "stream_v": stream_v, "short_taps": short_taps, "filters": filters, "live_mask": live_mask, "skip_gain": skip_gain}


def featurize(signal, weights):
    widened = signal.astype(jnp.float32)
    zero_col = jnp.zeros((widened.shape[0], 1), widened.dtype)
    back_one = jnp.concatenate((zero_col, widened[:, :-1]), axis=1)
    back_two = jnp.concatenate((zero_col, zero_col, widened[:, :-2]), axis=1)
    return weights[:, 0:1] * widened + weights[:, 1:2] * back_one + weights[:, 2:3] * back_two


def reference(stream_q, stream_k, stream_v, short_taps, filters, live_mask, skip_gain):
    block_width = 128
    block_count = stream_q.shape[0] // block_width
    group_index = (jnp.arange(C, dtype=jnp.int32) // (C // G)).astype(jnp.int32)

    def blocked(array):
        return array.reshape((block_count, block_width) + array.shape[1:])

    tap_blocks = jnp.swapaxes(short_taps.reshape(3, block_count, block_width, 3), 0, 1)

    def one_block(items):
        query_rows, key_rows, value_rows, weights, groups, alive_rows, gain_rows = items
        feat_query = featurize(query_rows, weights[0])
        feat_key = featurize(key_rows, weights[1])
        feat_value = featurize(value_rows, weights[2])
        product = (feat_key * feat_value).astype(jnp.bfloat16)
        widened = lax.optimization_barrier(product).astype(jnp.float32)
        chosen = filters[groups]
        padded = 2 * L
        spectrum = jnp.fft.rfft(widened, padded, axis=1) * jnp.fft.rfft(chosen, padded, axis=1)
        convolved = jnp.fft.irfft(spectrum, padded, axis=1)[:, :L].astype(jnp.bfloat16)
        conv_wide = lax.optimization_barrier(convolved).astype(jnp.float32)
        alive_wide = alive_rows[:, None].astype(jnp.float32)
        return (alive_wide * feat_query * (conv_wide + gain_rows[:, None] * widened)).astype(jnp.bfloat16)

    result = lax.map(one_block, (blocked(stream_q), blocked(stream_k), blocked(stream_v), tap_blocks,
                                 blocked(group_index), blocked(live_mask), blocked(skip_gain)))
    return result.reshape(stream_q.shape[0], stream_q.shape[1])
```

```python
import jax
import jax.numpy as jnp
from jax import lax
from jax.experimental import pallas as pl
from jax.experimental.pallas import tpu as pltpu
from jax.sharding import PartitionSpec as P

f32, bf16 = jnp.float32, jnp.bfloat16
PEERS = 32
OWN = 8
BLOCK = 512
LANES = 128
TILES = BLOCK // LANES
VMEM = pl.BlockSpec(memory_space=pltpu.VMEM)


def lanes_of(shape):
    return lax.broadcasted_iota(jnp.int32, shape, 1)


def rows_of(shape):
    return lax.broadcasted_iota(jnp.int32, shape, 0)


def features(signal, taps):
    return (
        taps[:, 0:1] * signal
        + taps[:, 1:2] * pltpu.roll(signal, 1, 1)
        + taps[:, 2:3] * pltpu.roll(signal, 2, 1)
    )


def message_kernel(q_ref, k_ref, v_ref, taps_ref, filt_ref, out_ref):
    lane = lanes_of((16, LANES))
    small_row = rows_of((8, LANES))
    for chunk in range(PEERS // 2):
        rows = slice(16 * chunk, 16 * chunk + 16)
        key = k_ref[rows, :].astype(f32)
        value = v_ref[rows, :].astype(f32)
        feat_key = features(key, taps_ref[1, rows, :])
        feat_value = features(value, taps_ref[2, rows, :])
        product = (feat_key * feat_value).astype(bf16)
        q_first = q_ref[rows, 0:LANES].astype(f32)
        q_last = q_ref[rows, BLOCK - LANES:].astype(f32)

        def ends(first, last, place):
            return pltpu.roll(jnp.where(lane >= 64, last, first), place, 1)

        k_ends = ends(key[:, 0:LANES], key[:, BLOCK - LANES:], 2)
        v_ends = ends(value[:, 0:LANES], value[:, BLOCK - LANES:], 6)
        q_ends = ends(q_first, q_last, 10)
        wide = jnp.where(small_row < 2, filt_ref[chunk:chunk + 1, 0:LANES],
                         jnp.where(small_row < 4, filt_ref[chunk:chunk + 1, LANES:2 * LANES],
                                   jnp.where(small_row < 6, filt_ref[chunk:chunk + 1, 2 * LANES:3 * LANES],
                                             filt_ref[chunk:chunk + 1, 3 * LANES:4 * LANES])))
        lags = jnp.where(small_row % 2 == 1, wide, pltpu.roll(wide, 64, 1))
        lags = jnp.concatenate((lags, lags), axis=0)
        edge = jnp.where(lane < 4, k_ends, jnp.where(lane < 8, v_ends, jnp.where(lane < 12, q_ends, lags)))
        edge = edge.astype(bf16)
        for half in range(2):
            peer = 2 * chunk + half
            part = slice(8 * half, 8 * half + 8)
            for tile in range(TILES):
                out_ref[peer, tile] = product[part, LANES * tile:LANES * (tile + 1)]
            out_ref[peer, TILES] = edge[part]


def gate_kernel(q_ref, k_ref, v_ref, taps_ref, live_ref, gain_ref, query_ref, skip_ref):
    for chunk in range(PEERS // 2):
        rows = slice(16 * chunk, 16 * chunk + 16)
        feat_query = features(q_ref[rows, :].astype(f32), taps_ref[0, rows, :])
        feat_key = features(k_ref[rows, :].astype(f32), taps_ref[1, rows, :])
        feat_value = features(v_ref[rows, :].astype(f32), taps_ref[2, rows, :])
        product = (feat_key * feat_value).astype(bf16).astype(f32)
        query_ref[rows, :] = live_ref[rows, :] * feat_query
        skip_ref[rows, :] = gain_ref[rows, :] * product


DEPTH = 4
STEPS = 64 // DEPTH


def conv_kernel(msg_ref, aux_ref, out_ref, lag_ref, toep_ref, rows_ref, left_ref, sum_ref):
    lane = lanes_of((256, LANES))
    pad = 8 * (DEPTH - 1)
    edge = msg_ref[:, TILES].astype(f32).reshape(256, LANES)
    lag_ref[...] = jnp.where(lane < 64, pltpu.roll(edge, 64, 1), pltpu.roll(edge, 255, 0))

    earlier = jnp.concatenate((jnp.zeros((8, LANES), f32), edge[:-8]), axis=0)
    joined = jnp.where(lane % 4 < 2, earlier, edge)

    def spread(index):
        return jnp.concatenate([aux_ref[index]] * PEERS, axis=0)

    feat = (
        spread(0) * joined
        + spread(1) * pltpu.roll(joined, 1, 1)
        + spread(2) * pltpu.roll(joined, 2, 1)
    )
    first_product = pltpu.roll(feat * pltpu.roll(feat, LANES - 4, 1), LANES - 2, 1)
    first_product = first_product.astype(bf16).astype(f32)
    first_query = pltpu.roll(feat, LANES - 10, 1)

    rows_ref[0:pad, :] = jnp.zeros((pad, 256), f32)
    for peer in range(PEERS):
        for tile in range(TILES):
            part = msg_ref[peer, tile].astype(f32)
            if tile == 0:
                part = jnp.where(lane[:8] < 2, first_product[8 * peer:8 * peer + 8], part)
            start = pad + 16 * peer + 8 * (tile // 2)
            rows_ref[start:start + 8, LANES * (tile % 2):LANES * (tile % 2 + 1)] = part
    for back in range(DEPTH):
        left_ref[:, 256 * back:256 * (back + 1)] = rows_ref[pad - 8 * back:pad - 8 * back + 512, :].astype(bf16)

    lower = lanes_of((LANES, LANES)) >= rows_of((LANES, LANES))
    toep_ref[0] = jnp.zeros((LANES, LANES), bf16)
    turned = jnp.zeros((LANES, LANES), f32)
    for step in range(STEPS):
        for e in range(2 * DEPTH * step, 2 * DEPTH * (step + 1)):
            before = turned
            row = jnp.broadcast_to(lag_ref[2 * e:2 * e + 1, :], (LANES, LANES))
            turned = pltpu.roll(row, 0, 1, stride=1, stride_axis=0)
            toep_ref[e + 1] = jnp.where(lower, turned, before).astype(bf16)
        first = DEPTH * step
        parts = []
        for back in range(DEPTH):
            for half in range(2):
                at = 1 + 2 * (first + back) - half
                parts.append(jnp.concatenate((toep_ref[at], toep_ref[at + 1]), axis=1))
        right = jnp.concatenate(parts, axis=0)
        offset = 8 * first
        got = jnp.dot(left_ref[0:512 - offset, :], right, preferred_element_type=f32)
        if step == 0:
            sum_ref[...] = got
        else:
            sum_ref[offset:, :] += got

    for peer in range(PEERS):
        for half in range(2):
            start = 16 * peer + 8 * half
            result = sum_ref[start:start + 8, :].astype(bf16)
            if half == 0:
                group = slice(8 * peer, 8 * peer + 8)
                head = result[:, 0:LANES].astype(f32)
                done = aux_ref[3] * first_query[group] * (head + aux_ref[4] * first_product[group])
                head = jnp.where(lane[:8] < 2, done, head).astype(bf16)
                out_ref[peer, :, 0:LANES] = head
                out_ref[peer, :, LANES:256] = result[:, LANES:]
            else:
                out_ref[peer, :, 256:512] = result


def shards(stream_q, stream_k, stream_v, short_taps, filters, live_mask, skip_gain):
    message = pl.pallas_call(
        message_kernel,
        out_shape=jax.ShapeDtypeStruct((PEERS, TILES + 1, 8, LANES), bf16),
        in_specs=[VMEM] * 5,
        out_specs=VMEM,
        compiler_params=pltpu.CompilerParams(vmem_limit_bytes=16 << 20),
        name="message",
    )(stream_q, stream_k, stream_v, short_taps, filters)
    arrived = lax.all_to_all(message, "seq", split_axis=0, concat_axis=0, tiled=True)

    live = live_mask.astype(f32)
    query, skip = pl.pallas_call(
        gate_kernel,
        out_shape=[jax.ShapeDtypeStruct((256, BLOCK), f32)] * 2,
        in_specs=[VMEM] * 6,
        out_specs=[VMEM] * 2,
        compiler_params=pltpu.CompilerParams(vmem_limit_bytes=16 << 20),
        cost_estimate=pl.CostEstimate(flops=4000000, bytes_accessed=2 << 20, transcendentals=0),
        name="gate",
    )(stream_q, stream_k, stream_v, short_taps, live[:, None], skip_gain[:, None])

    offset = lax.axis_index("seq") * OWN
    own_taps = lax.dynamic_slice_in_dim(short_taps, offset, OWN, 1)
    own_live = lax.dynamic_slice_in_dim(live, offset, OWN, 0)
    own_gain = lax.dynamic_slice_in_dim(skip_gain, offset, OWN, 0)
    by_tap = jnp.transpose(own_taps, (2, 1, 0))
    kind = lax.broadcasted_iota(jnp.int32, (3, OWN, LANES), 2) // 4
    weights = jnp.where(kind == 0, by_tap[:, :, 1:2], jnp.where(kind == 1, by_tap[:, :, 2:3], by_tap[:, :, 0:1]))
    aux = jnp.concatenate(
        (
            weights,
            jnp.broadcast_to(own_live[None, :, None], (1, OWN, LANES)),
            jnp.broadcast_to(own_gain[None, :, None], (1, OWN, LANES)),
        ),
        axis=0,
    )

    convolved = pl.pallas_call(
        conv_kernel,
        out_shape=jax.ShapeDtypeStruct((PEERS, OWN, BLOCK), bf16),
        in_specs=[VMEM] * 2,
        out_specs=VMEM,
        scratch_shapes=[
            pltpu.VMEM((256, LANES), f32),
            pltpu.VMEM((129, LANES, LANES), bf16),
            pltpu.VMEM((512 + 8 * (DEPTH - 1), 256), f32),
            pltpu.VMEM((512, 256 * DEPTH), bf16),
            pltpu.VMEM((512, 256), f32),
        ],
        compiler_params=pltpu.CompilerParams(vmem_limit_bytes=32 << 20),
        cost_estimate=pl.CostEstimate(flops=2300000000, bytes_accessed=1 << 20, transcendentals=0),
        name="conv",
    )(arrived, aux)
    back = lax.all_to_all(convolved, "seq", split_axis=0, concat_axis=0, tiled=True)
    back = back.reshape(256, BLOCK).astype(f32)
    column = lax.broadcasted_iota(jnp.int32, (256, BLOCK), 1)
    return jnp.where(column < 2, back, query * (back + skip)).astype(bf16)


def solution(mesh):
    in_specs = (
        P("tp", "seq"),
        P("tp", "seq"),
        P("tp", "seq"),
        P(None, "tp", None),
        P("tp", "seq"),
        P("tp"),
        P("tp"),
    )
    return jax.shard_map(shards, mesh=mesh, in_specs=in_specs, out_specs=P("tp", "seq"), check_vma=False)
```

```python
import jax
import jax.numpy as jnp
from jax import lax
from jax.experimental import pallas as pl
from jax.experimental.pallas import tpu as pltpu
from jax.sharding import PartitionSpec as P

f32, bf16 = jnp.float32, jnp.bfloat16
PEERS = 32
OWN = 8
BLOCK = 512
LANES = 128
TILES = BLOCK // LANES
FIRST_OUT, FIRST_BACK = 22, 16
ORDER_OUT = [(place + FIRST_OUT) % PEERS for place in range(PEERS)]
ORDER_BACK = [(place + FIRST_BACK) % PEERS for place in range(PEERS)]


def place_there(group):
    return (group + FIRST_BACK - FIRST_OUT) % PEERS


def place_from(block):
    return (block - FIRST_OUT) % PEERS


def place_back(block):
    return (block - FIRST_BACK) % PEERS


def runs(places):
    found = []
    for place in sorted(places):
        if found and found[-1].stop == place:
            found[-1] = slice(found[-1].start, place + 1)
        else:
            found.append(slice(place, place + 1))
    return found


VMEM = pl.BlockSpec(memory_space=pltpu.VMEM)
HBM = pl.BlockSpec(memory_space=pltpu.HBM)


def lanes_of(shape):
    return lax.broadcasted_iota(jnp.int32, shape, 1)


def rows_of(shape):
    return lax.broadcasted_iota(jnp.int32, shape, 0)


def features(signal, taps):
    return (
        taps[:, 0:1] * signal
        + taps[:, 1:2] * pltpu.roll(signal, 1, 1)
        + taps[:, 2:3] * pltpu.roll(signal, 2, 1)
    )


def columns_of(rows):
    spare = 16 - sum(row.shape[0] for row in rows)
    return jnp.transpose(jnp.concatenate(list(rows) + [jnp.zeros((spare, 256), f32)], axis=0))


PARTS = 4
ROWS = 256 // PARTS


def message_kernel(q_hbm, k_hbm, v_hbm, taps_hbm, filt_hbm, out_hbm, qf, ql, kk, vv, taps_ref, filt_ref, out_ref, sems, out_sems):
    small = [
        pltpu.make_async_copy(taps_hbm, taps_ref, sems.at[0]),
        pltpu.make_async_copy(filt_hbm, filt_ref, sems.at[1]),
        pltpu.make_async_copy(q_hbm.at[:, 0:LANES], qf, sems.at[2]),
        pltpu.make_async_copy(q_hbm.at[:, BLOCK - LANES:], ql, sems.at[3]),
    ]
    small[0].start()
    loads = []
    for part in range(PARTS):
        span = slice(ROWS * part, ROWS * (part + 1))
        loads.append(
            (
                pltpu.make_async_copy(k_hbm.at[span], kk.at[span], sems.at[4 + 2 * part]),
                pltpu.make_async_copy(v_hbm.at[span], vv.at[span], sems.at[5 + 2 * part]),
            )
        )
        for copy in loads[-1]:
            copy.start()
        if part == 0:
            for copy in small[1:]:
                copy.start()
    small[0].wait()
    taps = columns_of((taps_ref[1], taps_ref[2]))
    lane = lanes_of((16, LANES))
    small_row = rows_of((8, LANES))
    stores = []
    for part in range(PARTS):
        for copy in loads[part]:
            copy.wait()
        if part == 0:
            for copy in small[1:]:
                copy.wait()
        for chunk in range(part * ROWS // 16, (part + 1) * ROWS // 16):
            rows = slice(16 * chunk, 16 * chunk + 16)
            key = kk[rows, :].astype(f32)
            value = vv[rows, :].astype(f32)
            feat_key = features(key, taps[rows, 0:3])
            feat_value = features(value, taps[rows, 3:6])
            product = (feat_key * feat_value).astype(bf16)

            def ends(first, last, place):
                return pltpu.roll(jnp.where(lane >= 64, last, first), place, 1)

            k_ends = ends(key[:, 0:LANES], key[:, BLOCK - LANES:], 2)
            v_ends = ends(value[:, 0:LANES], value[:, BLOCK - LANES:], 6)
            q_ends = ends(qf[rows, :].astype(f32), ql[rows, :].astype(f32), 10)
            wide = jnp.where(small_row < 2, filt_ref[chunk:chunk + 1, 0:LANES],
                             jnp.where(small_row < 4, filt_ref[chunk:chunk + 1, LANES:2 * LANES],
                                       jnp.where(small_row < 6, filt_ref[chunk:chunk + 1, 2 * LANES:3 * LANES],
                                                 filt_ref[chunk:chunk + 1, 3 * LANES:4 * LANES])))
            lags = jnp.where(small_row % 2 == 1, wide, pltpu.roll(wide, 64, 1))
            lags = jnp.concatenate((lags, lags), axis=0)
            edge = jnp.where(lane < 4, k_ends, jnp.where(lane < 8, v_ends, jnp.where(lane < 12, q_ends, lags)))
            edge = edge.astype(bf16)
            for half in range(2):
                peer = 2 * chunk + half
                piece = slice(8 * half, 8 * half + 8)
                for tile in range(TILES):
                    out_ref[place_there(peer), tile] = product[piece, LANES * tile:LANES * (tile + 1)]
                out_ref[place_there(peer), TILES] = edge[piece]
        for span in runs([place_there(part * PEERS // PARTS + peer) for peer in range(PEERS // PARTS)]):
            stores.append(pltpu.make_async_copy(out_ref.at[span], out_hbm.at[span], out_sems.at[len(stores)]))
            stores[-1].start()
    for copy in stores:
        copy.wait()


def gate_kernel(q_ref, k_ref, v_ref, taps_ref, live_ref, gain_ref, query_ref, skip_ref, aux_ref, table_ref):
    table_ref[...] = columns_of(
        (taps_ref[0], taps_ref[1], taps_ref[2], live_ref[...].astype(f32), gain_ref[...])
    )
    place = lax.rem(lax.axis_index("seq") + PEERS - FIRST_BACK, PEERS)
    own = table_ref[pl.ds(pl.multiple_of(place * OWN, OWN), OWN), :]
    kind = lanes_of((OWN, LANES)) // 4
    for tap in range(3):
        aux_ref[tap] = jnp.where(
            kind == 0, own[:, 3 + tap:4 + tap], jnp.where(kind == 1, own[:, 6 + tap:7 + tap], own[:, tap:tap + 1])
        )
    for place in range(2):
        aux_ref[3 + place] = jnp.broadcast_to(own[:, 9 + place:10 + place], (OWN, LANES))
    for chunk in range(PEERS // 2):
        rows = slice(16 * chunk, 16 * chunk + 16)
        taps = table_ref[rows, :]
        feat_query = features(q_ref[rows, :].astype(f32), taps[:, 0:3])
        feat_key = features(k_ref[rows, :].astype(f32), taps[:, 3:6])
        feat_value = features(v_ref[rows, :].astype(f32), taps[:, 6:9])
        product = (feat_key * feat_value).astype(bf16).astype(f32)
        query_ref[rows, :] = taps[:, 9:10] * feat_query
        skip_ref[rows, :] = taps[:, 10:11] * product


DEPTH = 4
STEPS = 64 // DEPTH


def conv_kernel(msg_ref, aux_ref, out_hbm, lag_ref, toep_ref, rows_ref, left_ref, sum_ref, out_ref, sems):
    lane = lanes_of((256, LANES))
    pad = 8 * (DEPTH - 1)
    edge = jnp.concatenate([msg_ref[place_from(block), TILES].astype(f32) for block in range(PEERS)], axis=0)
    lag_ref[...] = jnp.where(lane < 64, pltpu.roll(edge, 64, 1), pltpu.roll(edge, 255, 0))

    earlier = jnp.concatenate((jnp.zeros((8, LANES), f32), edge[:-8]), axis=0)
    joined = jnp.where(lane % 4 < 2, earlier, edge)

    def spread(index):
        return jnp.concatenate([aux_ref[index]] * PEERS, axis=0)

    feat = (
        spread(0) * joined
        + spread(1) * pltpu.roll(joined, 1, 1)
        + spread(2) * pltpu.roll(joined, 2, 1)
    )
    first_product = pltpu.roll(feat * pltpu.roll(feat, LANES - 4, 1), LANES - 2, 1)
    first_product = first_product.astype(bf16).astype(f32)
    first_query = pltpu.roll(feat, LANES - 10, 1)

    rows_ref[0:pad, :] = jnp.zeros((pad, 256), f32)
    for peer in range(PEERS):
        for tile in range(TILES):
            part = msg_ref[place_from(peer), tile].astype(f32)
            if tile == 0:
                part = jnp.where(lane[:8] < 2, first_product[8 * peer:8 * peer + 8], part)
            start = pad + 16 * peer + 8 * (tile // 2)
            rows_ref[start:start + 8, LANES * (tile % 2):LANES * (tile % 2 + 1)] = part
    for back in range(DEPTH):
        left_ref[:, 256 * back:256 * (back + 1)] = rows_ref[pad - 8 * back:pad - 8 * back + 512, :].astype(bf16)

    lower = lanes_of((LANES, LANES)) >= rows_of((LANES, LANES))
    toep_ref[0] = jnp.zeros((LANES, LANES), bf16)
    turned = jnp.zeros((LANES, LANES), f32)
    stores = []
    for step in range(STEPS):
        for e in range(2 * DEPTH * step, 2 * DEPTH * (step + 1)):
            before = turned
            row = jnp.broadcast_to(lag_ref[2 * e:2 * e + 1, :], (LANES, LANES))
            turned = pltpu.roll(row, 0, 1, stride=1, stride_axis=0)
            toep_ref[e + 1] = jnp.where(lower, turned, before).astype(bf16)
        first = DEPTH * step
        parts = []
        for back in range(DEPTH):
            for half in range(2):
                at = 1 + 2 * (first + back) - half
                parts.append(jnp.concatenate((toep_ref[at], toep_ref[at + 1]), axis=1))
        right = jnp.concatenate(parts, axis=0)
        offset = 8 * first
        got = jnp.dot(left_ref[0:512 - offset, :], right, preferred_element_type=f32)
        if step == 0:
            sum_ref[...] = got
        else:
            sum_ref[offset:, :] += got

        for peer in range(DEPTH // 2 * step, DEPTH // 2 * (step + 1)):
            group = slice(8 * peer, 8 * peer + 8)
            result = sum_ref[16 * peer:16 * peer + 16, :].astype(bf16)
            head = result[0:8, 0:LANES].astype(f32)
            done = aux_ref[3] * first_query[group] * (head + aux_ref[4] * first_product[group])
            out_ref[place_back(peer), :, 0:LANES] = jnp.where(lane[:8] < 2, done, head).astype(bf16)
            out_ref[place_back(peer), :, LANES:256] = result[0:8, LANES:]
            out_ref[place_back(peer), :, 256:512] = result[8:16]
        if step % 2:
            for span in runs([place_back(DEPTH // 2 * (step - 1) + peer) for peer in range(DEPTH)]):
                stores.append(pltpu.make_async_copy(out_ref.at[span], out_hbm.at[span], sems.at[len(stores)]))
                stores[-1].start()
    for copy in stores:
        copy.wait()


def shards(stream_q, stream_k, stream_v, short_taps, filters, live_mask, skip_gain):
    taps_wide = jnp.transpose(short_taps, (0, 2, 1))
    message = pl.pallas_call(
        message_kernel,
        out_shape=jax.ShapeDtypeStruct((PEERS, TILES + 1, 8, LANES), bf16),
        in_specs=[HBM] * 5,
        out_specs=HBM,
        scratch_shapes=[
            pltpu.VMEM((256, LANES), bf16),
            pltpu.VMEM((256, LANES), bf16),
            pltpu.VMEM((256, BLOCK), bf16),
            pltpu.VMEM((256, BLOCK), bf16),
            pltpu.VMEM((3, 3, 256), f32),
            pltpu.VMEM((16, BLOCK), f32),
            pltpu.VMEM((PEERS, TILES + 1, 8, LANES), bf16),
            pltpu.SemaphoreType.DMA((4 + 2 * PARTS,)),
            pltpu.SemaphoreType.DMA((2 * PARTS,)),
        ],
        name="message",
    )(stream_q, stream_k, stream_v, taps_wide, filters)
    arrived = lax.all_to_all(message, "seq", split_axis=0, concat_axis=0, tiled=True, axis_index_groups=[ORDER_OUT])

    query, skip, aux = pl.pallas_call(
        gate_kernel,
        out_shape=[jax.ShapeDtypeStruct((256, BLOCK), f32)] * 2 + [jax.ShapeDtypeStruct((5, OWN, LANES), f32)],
        in_specs=[VMEM] * 6,
        out_specs=[VMEM] * 3,
        scratch_shapes=[pltpu.VMEM((256, 16), f32)],
        compiler_params=pltpu.CompilerParams(vmem_limit_bytes=16 << 20),
        cost_estimate=pl.CostEstimate(flops=4000000, bytes_accessed=2 << 20, transcendentals=0),
        name="gate",
    )(stream_q, stream_k, stream_v, taps_wide, live_mask[None, :], skip_gain[None, :])

    convolved = pl.pallas_call(
        conv_kernel,
        out_shape=jax.ShapeDtypeStruct((PEERS, OWN, BLOCK), bf16),
        in_specs=[VMEM] * 2,
        out_specs=HBM,
        scratch_shapes=[
            pltpu.VMEM((256, LANES), f32),
            pltpu.VMEM((129, LANES, LANES), bf16),
            pltpu.VMEM((512 + 8 * (DEPTH - 1), 256), f32),
            pltpu.VMEM((512, 256 * DEPTH), bf16),
            pltpu.VMEM((512, 256), f32),
            pltpu.VMEM((PEERS, OWN, BLOCK), bf16),
            pltpu.SemaphoreType.DMA((STEPS,)),
        ],
        compiler_params=pltpu.CompilerParams(vmem_limit_bytes=32 << 20),
        cost_estimate=pl.CostEstimate(flops=2300000000, bytes_accessed=1 << 20, transcendentals=0),
        name="conv",
    )(arrived, aux)
    back = lax.all_to_all(convolved, "seq", split_axis=0, concat_axis=0, tiled=True, axis_index_groups=[ORDER_BACK])
    back = back.reshape(256, BLOCK).astype(f32)
    column = lax.broadcasted_iota(jnp.int32, (256, BLOCK), 1)
    return jnp.where(column < 2, back, query * (back + skip)).astype(bf16)


def solution(mesh):
    in_specs = (
        P("tp", "seq"),
        P("tp", "seq"),
        P("tp", "seq"),
        P(None, "tp", None),
        P("tp", "seq"),
        P("tp"),
        P("tp"),
    )
    return jax.shard_map(shards, mesh=mesh, in_specs=in_specs, out_specs=P("tp", "seq"), check_vma=False)
```

```python
import jax
import jax.numpy as jnp
from jax import lax
from jax.experimental import pallas as pl
from jax.experimental.pallas import tpu as pltpu
from jax.sharding import PartitionSpec as P

f32, bf16 = jnp.float32, jnp.bfloat16
PEERS = 32
OWN = 8
BLOCK = 512
LANES = 128
TILES = BLOCK // LANES
FIRST_OUT, FIRST_BACK = 22, 16
ORDER_OUT = [(FIRST_OUT + place) % PEERS for place in range(PEERS)]
ORDER_BACK = [(FIRST_BACK + place) % PEERS for place in range(PEERS)]


def own_group(index):
    return lax.rem(index + PEERS - FIRST_BACK, PEERS)


def place_there(group):
    return ORDER_OUT.index(ORDER_BACK[group])


def place_from(block):
    return ORDER_OUT.index(block)


def place_back(block):
    return ORDER_BACK.index(block)


VMEM = pl.BlockSpec(memory_space=pltpu.VMEM)
HBM = pl.BlockSpec(memory_space=pltpu.HBM)


def lanes_of(shape):
    return lax.broadcasted_iota(jnp.int32, shape, 1)


def rows_of(shape):
    return lax.broadcasted_iota(jnp.int32, shape, 0)


def features(signal, taps):
    return (
        taps[:, 0:1] * signal
        + taps[:, 1:2] * pltpu.roll(signal, 1, 1)
        + taps[:, 2:3] * pltpu.roll(signal, 2, 1)
    )


def columns_of(rows):
    spare = 16 - sum(row.shape[0] for row in rows)
    return jnp.transpose(jnp.concatenate(list(rows) + [jnp.zeros((spare, 256), f32)], axis=0))


def spread_rows(rows):
    count = sum(row.shape[0] for row in rows)
    values = jnp.concatenate(list(rows) + [jnp.zeros((8 - count, 256), f32)], axis=0)
    terms = []
    for _ in range(3):
        terms.append(values.astype(bf16).astype(f32))
        values = values - terms[-1]
    shape = (24, LANES * count)
    pick = (rows_of(shape) % 8 == lanes_of(shape) // LANES).astype(bf16)
    columns = jnp.transpose(jnp.concatenate(terms, axis=0)).astype(bf16)
    return jnp.dot(columns, pick, preferred_element_type=f32)


STORES = 4


def message_kernel(q_hbm, k_hbm, v_hbm, taps_hbm, filt_hbm, out_hbm, qf, ql, kk, vv, taps_ref, filt_ref, wide_ref, out_ref, sems, out_sems):
    loads = [
        pltpu.make_async_copy(taps_hbm, taps_ref, sems.at[0]),
        pltpu.make_async_copy(k_hbm, kk, sems.at[1]),
        pltpu.make_async_copy(v_hbm, vv, sems.at[2]),
        pltpu.make_async_copy(filt_hbm, filt_ref, sems.at[3]),
        pltpu.make_async_copy(q_hbm.at[:, 0:LANES], qf, sems.at[4]),
        pltpu.make_async_copy(q_hbm.at[:, BLOCK - LANES:], ql, sems.at[5]),
    ]
    for copy in loads:
        copy.start()
    loads[0].wait()
    wide_ref[...] = spread_rows((taps_ref[1], taps_ref[2]))
    for copy in loads[1:]:
        copy.wait()
    lane = lanes_of((16, LANES))
    small_row = rows_of((8, LANES))
    chunks = sorted(range(PEERS // 2), key=lambda chunk: place_there(2 * chunk))
    stores = []
    for done, chunk in enumerate(chunks):
        rows = slice(16 * chunk, 16 * chunk + 16)
        key = kk[rows, :].astype(f32)
        value = vv[rows, :].astype(f32)

        def features(signal, first):
            taps = [
                jnp.concatenate([wide_ref[rows, LANES * at:LANES * (at + 1)]] * TILES, axis=1)
                for at in range(first, first + 3)
            ]
            return taps[0] * signal + taps[1] * pltpu.roll(signal, 1, 1) + taps[2] * pltpu.roll(signal, 2, 1)

        product = features(key, 0) * features(value, 3)

        def ends(first, last, place):
            return pltpu.roll(jnp.where(lane >= 64, last, first), place, 1)

        k_ends = ends(key[:, 0:LANES], key[:, BLOCK - LANES:], 2)
        v_ends = ends(value[:, 0:LANES], value[:, BLOCK - LANES:], 6)
        q_ends = ends(qf[rows, :].astype(f32), ql[rows, :].astype(f32), 10)
        wide = jnp.where(small_row < 2, filt_ref[chunk:chunk + 1, 0:LANES],
                         jnp.where(small_row < 4, filt_ref[chunk:chunk + 1, LANES:2 * LANES],
                                   jnp.where(small_row < 6, filt_ref[chunk:chunk + 1, 2 * LANES:3 * LANES],
                                             filt_ref[chunk:chunk + 1, 3 * LANES:4 * LANES])))
        lags = jnp.where(small_row % 2 == 1, wide, pltpu.roll(wide, 64, 1))
        lags = jnp.concatenate((lags, lags), axis=0)
        edge = jnp.where(lane < 4, k_ends, jnp.where(lane < 8, v_ends, jnp.where(lane < 12, q_ends, lags)))
        for half in range(2):
            place = place_there(2 * chunk + half)
            piece = slice(8 * half, 8 * half + 8)
            for tile in range(TILES):
                out_ref[place, tile] = product[piece, LANES * tile:LANES * (tile + 1)].astype(bf16)
            out_ref[place, TILES] = edge[piece].astype(bf16)
        if (done + 1) % (len(chunks) // STORES) == 0:
            span = slice(PEERS // STORES * len(stores), PEERS // STORES * (len(stores) + 1))
            stores.append(pltpu.make_async_copy(out_ref.at[span], out_hbm.at[span], out_sems.at[len(stores)]))
            stores[-1].start()
    for copy in stores:
        copy.wait()


def gate_kernel(q_ref, k_ref, v_ref, taps_ref, live_ref, gain_ref, query_ref, skip_ref, aux_ref, table_ref):
    table_ref[...] = columns_of(
        (taps_ref[0], taps_ref[1], taps_ref[2], live_ref[...].astype(f32), gain_ref[...])
    )
    own = table_ref[pl.ds(pl.multiple_of(own_group(lax.axis_index("seq")) * OWN, OWN), OWN), :]
    kind = lanes_of((OWN, LANES)) // 4
    for tap in range(3):
        aux_ref[tap] = jnp.where(
            kind == 0, own[:, 3 + tap:4 + tap], jnp.where(kind == 1, own[:, 6 + tap:7 + tap], own[:, tap:tap + 1])
        )
    for place in range(2):
        aux_ref[3 + place] = jnp.broadcast_to(own[:, 9 + place:10 + place], (OWN, LANES))
    for chunk in range(PEERS // 2):
        rows = slice(16 * chunk, 16 * chunk + 16)
        taps = table_ref[rows, :]
        feat_query = features(q_ref[rows, :].astype(f32), taps[:, 0:3])
        feat_key = features(k_ref[rows, :].astype(f32), taps[:, 3:6])
        feat_value = features(v_ref[rows, :].astype(f32), taps[:, 6:9])
        product = (feat_key * feat_value).astype(bf16).astype(f32)
        finished = lanes_of((16, BLOCK)) < 2
        query_ref[rows, :] = jnp.where(finished, 1.0, taps[:, 9:10] * feat_query)
        skip_ref[rows, :] = jnp.where(finished, 0.0, taps[:, 10:11] * product)


DEPTH = 4
STEPS = 64 // DEPTH


def conv_kernel(msg_ref, aux_ref, out_ref, lag_ref, toep_ref, rows_ref, left_ref, sum_ref):
    lane = lanes_of((256, LANES))
    pad = 8 * (DEPTH - 1)
    edge = jnp.concatenate([msg_ref[place_from(block), TILES].astype(f32) for block in range(PEERS)], axis=0)
    lag_ref[...] = jnp.where(lane < 64, pltpu.roll(edge, 64, 1), pltpu.roll(edge, 255, 0))

    earlier = jnp.concatenate((jnp.zeros((8, LANES), f32), edge[:-8]), axis=0)
    joined = jnp.where(lane % 4 < 2, earlier, edge)

    def spread(index):
        return jnp.concatenate([aux_ref[index]] * PEERS, axis=0)

    feat = (
        spread(0) * joined
        + spread(1) * pltpu.roll(joined, 1, 1)
        + spread(2) * pltpu.roll(joined, 2, 1)
    )
    first_product = pltpu.roll(feat * pltpu.roll(feat, LANES - 4, 1), LANES - 2, 1)
    first_product = first_product.astype(bf16).astype(f32)
    first_query = pltpu.roll(feat, LANES - 10, 1)

    rows_ref[0:pad, :] = jnp.zeros((pad, 256), f32)
    for peer in range(PEERS):
        for tile in range(TILES):
            part = msg_ref[place_from(peer), tile].astype(f32)
            if tile == 0:
                part = jnp.where(lane[:8] < 2, first_product[8 * peer:8 * peer + 8], part)
            start = pad + 16 * peer + 8 * (tile // 2)
            rows_ref[start:start + 8, LANES * (tile % 2):LANES * (tile % 2 + 1)] = part
    for back in range(DEPTH):
        left_ref[:, 256 * back:256 * (back + 1)] = rows_ref[pad - 8 * back:pad - 8 * back + 512, :].astype(bf16)

    lower = lanes_of((LANES, LANES)) >= rows_of((LANES, LANES))
    toep_ref[0] = jnp.zeros((LANES, LANES), bf16)
    turned = jnp.zeros((LANES, LANES), f32)
    for step in range(STEPS):
        for e in range(2 * DEPTH * step, 2 * DEPTH * (step + 1)):
            before = turned
            row = jnp.broadcast_to(lag_ref[2 * e:2 * e + 1, :], (LANES, LANES))
            turned = pltpu.roll(row, 0, 1, stride=1, stride_axis=0)
            toep_ref[e + 1] = jnp.where(lower, turned, before).astype(bf16)
        first = DEPTH * step
        parts = []
        for back in range(DEPTH):
            for half in range(2):
                at = 1 + 2 * (first + back) - half
                parts.append(jnp.concatenate((toep_ref[at], toep_ref[at + 1]), axis=1))
        right = jnp.concatenate(parts, axis=0)
        offset = 8 * first
        got = jnp.dot(left_ref[0:512 - offset, :], right, preferred_element_type=f32)
        if step == 0:
            sum_ref[...] = got
        else:
            sum_ref[offset:, :] += got

        for peer in range(DEPTH // 2 * step, DEPTH // 2 * (step + 1)):
            group = slice(8 * peer, 8 * peer + 8)
            result = sum_ref[16 * peer:16 * peer + 16, :].astype(bf16)
            head = result[0:8, 0:LANES].astype(f32)
            done = aux_ref[3] * first_query[group] * (head + aux_ref[4] * first_product[group])
            out_ref[place_back(peer), :, 0:LANES] = jnp.where(lane[:8] < 2, done, head).astype(bf16)
            out_ref[place_back(peer), :, LANES:256] = result[0:8, LANES:]
            out_ref[place_back(peer), :, 256:512] = result[8:16]


def shards(stream_q, stream_k, stream_v, short_taps, filters, live_mask, skip_gain):
    taps_wide = jnp.transpose(short_taps, (0, 2, 1))
    message = pl.pallas_call(
        message_kernel,
        out_shape=jax.ShapeDtypeStruct((PEERS, TILES + 1, 8, LANES), bf16),
        in_specs=[HBM] * 5,
        out_specs=HBM,
        scratch_shapes=[
            pltpu.VMEM((256, LANES), bf16),
            pltpu.VMEM((256, LANES), bf16),
            pltpu.VMEM((256, BLOCK), bf16),
            pltpu.VMEM((256, BLOCK), bf16),
            pltpu.VMEM((3, 3, 256), f32),
            pltpu.VMEM((16, BLOCK), f32),
            pltpu.VMEM((256, 6 * LANES), f32),
            pltpu.VMEM((PEERS, TILES + 1, 8, LANES), bf16),
            pltpu.SemaphoreType.DMA((6,)),
            pltpu.SemaphoreType.DMA((STORES,)),
        ],
        name="message",
    )(stream_q, stream_k, stream_v, taps_wide, filters)
    arrived = lax.all_to_all(message, "seq", split_axis=0, concat_axis=0, tiled=True, axis_index_groups=[ORDER_OUT])

    query, skip, aux = pl.pallas_call(
        gate_kernel,
        out_shape=[jax.ShapeDtypeStruct((256, BLOCK), f32)] * 2 + [jax.ShapeDtypeStruct((5, OWN, LANES), f32)],
        in_specs=[VMEM] * 6,
        out_specs=[VMEM] * 3,
        scratch_shapes=[pltpu.VMEM((256, 16), f32)],
        compiler_params=pltpu.CompilerParams(vmem_limit_bytes=16 << 20),
        cost_estimate=pl.CostEstimate(flops=4000000, bytes_accessed=2 << 20, transcendentals=0),
        name="gate",
    )(stream_q, stream_k, stream_v, taps_wide, live_mask[None, :], skip_gain[None, :])

    convolved = pl.pallas_call(
        conv_kernel,
        out_shape=jax.ShapeDtypeStruct((PEERS, OWN, BLOCK), bf16),
        in_specs=[VMEM] * 2,
        out_specs=VMEM,
        scratch_shapes=[
            pltpu.VMEM((256, LANES), f32),
            pltpu.VMEM((129, LANES, LANES), bf16),
            pltpu.VMEM((512 + 8 * (DEPTH - 1), 256), f32),
            pltpu.VMEM((512, 256 * DEPTH), bf16),
            pltpu.VMEM((512, 256), f32),
        ],
        compiler_params=pltpu.CompilerParams(vmem_limit_bytes=32 << 20),
        cost_estimate=pl.CostEstimate(flops=2300000000, bytes_accessed=1 << 20, transcendentals=0),
        name="conv",
    )(arrived, aux)
    back = lax.all_to_all(convolved, "seq", split_axis=0, concat_axis=0, tiled=True, axis_index_groups=[ORDER_BACK])
    return (query * (back.reshape(256, BLOCK).astype(f32) + skip)).astype(bf16)


def solution(mesh):
    in_specs = (
        P("tp", "seq"),
        P("tp", "seq"),
        P("tp", "seq"),
        P(None, "tp", None),
        P("tp", "seq"),
        P("tp"),
        P("tp"),
    )
    return jax.shard_map(shards, mesh=mesh, in_specs=in_specs, out_specs=P("tp", "seq"), check_vma=False)
```

```python
import jax
import jax.numpy as jnp
from jax import lax
from jax.experimental import pallas as pl
from jax.experimental.pallas import tpu as pltpu
from jax.sharding import PartitionSpec as P

f32, bf16 = jnp.float32, jnp.bfloat16
PEERS = 32
OWN = 8
BLOCK = 512
LANES = 128
TILES = BLOCK // LANES
FIRST_OUT, FIRST_BACK = 23, 17
ORDER_OUT, ORDER_BACK = (
    [first] + [index for index in range(PEERS) if index != first] for first in (FIRST_OUT, FIRST_BACK)
)


def own_group(index):
    return jnp.where(index == FIRST_BACK, 0, jnp.where(index < FIRST_BACK, index + 1, index))


def place_there(group):
    return ORDER_OUT.index(ORDER_BACK[group])


def place_from(block):
    return ORDER_OUT.index(block)


def place_back(block):
    return ORDER_BACK.index(block)


VMEM = pl.BlockSpec(memory_space=pltpu.VMEM)
HBM = pl.BlockSpec(memory_space=pltpu.HBM)


def lanes_of(shape):
    return lax.broadcasted_iota(jnp.int32, shape, 1)


def rows_of(shape):
    return lax.broadcasted_iota(jnp.int32, shape, 0)


def features(signal, taps):
    return (
        taps[:, 0:1] * signal
        + taps[:, 1:2] * pltpu.roll(signal, 1, 1)
        + taps[:, 2:3] * pltpu.roll(signal, 2, 1)
    )


def columns_of(rows):
    spare = 16 - sum(row.shape[0] for row in rows)
    return jnp.transpose(jnp.concatenate(list(rows) + [jnp.zeros((spare, 256), f32)], axis=0))


def spread_rows(rows):
    count = sum(row.shape[0] for row in rows)
    values = jnp.concatenate(list(rows) + [jnp.zeros((8 - count, 256), f32)], axis=0)
    terms = []
    for _ in range(3):
        terms.append(values.astype(bf16).astype(f32))
        values = values - terms[-1]
    shape = (24, LANES * count)
    pick = (rows_of(shape) % 8 == lanes_of(shape) // LANES).astype(bf16)
    columns = jnp.transpose(jnp.concatenate(terms, axis=0)).astype(bf16)
    return jnp.dot(columns, pick, preferred_element_type=f32)


STORES = 4


def message_kernel(q_hbm, k_hbm, v_hbm, taps_hbm, filt_hbm, out_hbm, qf, ql, kk, vv, taps_ref, filt_ref, wide_ref, out_ref, sems, out_sems):
    loads = [
        pltpu.make_async_copy(taps_hbm, taps_ref, sems.at[0]),
        pltpu.make_async_copy(k_hbm, kk, sems.at[1]),
        pltpu.make_async_copy(v_hbm, vv, sems.at[2]),
        pltpu.make_async_copy(filt_hbm, filt_ref, sems.at[3]),
        pltpu.make_async_copy(q_hbm.at[:, 0:LANES], qf, sems.at[4]),
        pltpu.make_async_copy(q_hbm.at[:, BLOCK - LANES:], ql, sems.at[5]),
    ]
    for copy in loads:
        copy.start()
    loads[0].wait()
    wide_ref[...] = spread_rows((taps_ref[1], taps_ref[2]))
    for copy in loads[1:]:
        copy.wait()
    lane = lanes_of((16, LANES))
    small_row = rows_of((8, LANES))
    group_at = {place_there(group): group for group in range(PEERS)}
    chunks = list(dict.fromkeys(group_at[place] // 2 for place in range(PEERS)))
    stores = []
    for done, chunk in enumerate(chunks):
        rows = slice(16 * chunk, 16 * chunk + 16)
        key = kk[rows, :].astype(f32)
        value = vv[rows, :].astype(f32)

        def features(signal, first):
            taps = [
                jnp.concatenate([wide_ref[rows, LANES * at:LANES * (at + 1)]] * TILES, axis=1)
                for at in range(first, first + 3)
            ]
            return taps[0] * signal + taps[1] * pltpu.roll(signal, 1, 1) + taps[2] * pltpu.roll(signal, 2, 1)

        product = features(key, 0) * features(value, 3)

        def ends(first, last, place):
            return pltpu.roll(jnp.where(lane >= 64, last, first), place, 1)

        k_ends = ends(key[:, 0:LANES], key[:, BLOCK - LANES:], 2)
        v_ends = ends(value[:, 0:LANES], value[:, BLOCK - LANES:], 6)
        q_ends = ends(qf[rows, :].astype(f32), ql[rows, :].astype(f32), 10)
        wide = jnp.where(small_row < 2, filt_ref[chunk:chunk + 1, 0:LANES],
                         jnp.where(small_row < 4, filt_ref[chunk:chunk + 1, LANES:2 * LANES],
                                   jnp.where(small_row < 6, filt_ref[chunk:chunk + 1, 2 * LANES:3 * LANES],
                                             filt_ref[chunk:chunk + 1, 3 * LANES:4 * LANES])))
        lags = jnp.where(small_row % 2 == 1, wide, pltpu.roll(wide, 64, 1))
        lags = jnp.concatenate((lags, lags), axis=0)
        edge = jnp.where(lane < 4, k_ends, jnp.where(lane < 8, v_ends, jnp.where(lane < 12, q_ends, lags)))
        for half in range(2):
            place = place_there(2 * chunk + half)
            piece = slice(8 * half, 8 * half + 8)
            for tile in range(TILES):
                out_ref[place, tile] = product[piece, LANES * tile:LANES * (tile + 1)].astype(bf16)
            out_ref[place, TILES] = edge[piece].astype(bf16)
        full = {place_there(2 * chunk + half) for chunk in chunks[:done + 1] for half in range(2)}
        while len(stores) < STORES:
            span = slice(PEERS // STORES * len(stores), PEERS // STORES * (len(stores) + 1))
            if not full.issuperset(range(span.start, span.stop)):
                break
            stores.append(pltpu.make_async_copy(out_ref.at[span], out_hbm.at[span], out_sems.at[len(stores)]))
            stores[-1].start()
    assert len(stores) == STORES
    for copy in stores:
        copy.wait()


def gate_kernel(q_ref, k_ref, v_ref, taps_ref, live_ref, gain_ref, query_ref, skip_ref, aux_ref, table_ref):
    table_ref[...] = columns_of(
        (taps_ref[0], taps_ref[1], taps_ref[2], live_ref[...].astype(f32), gain_ref[...])
    )
    own = table_ref[pl.ds(pl.multiple_of(own_group(lax.axis_index("seq")) * OWN, OWN), OWN), :]
    kind = lanes_of((OWN, LANES)) // 4
    for tap in range(3):
        aux_ref[tap] = jnp.where(
            kind == 0, own[:, 3 + tap:4 + tap], jnp.where(kind == 1, own[:, 6 + tap:7 + tap], own[:, tap:tap + 1])
        )
    for place in range(2):
        aux_ref[3 + place] = jnp.broadcast_to(own[:, 9 + place:10 + place], (OWN, LANES))
    for chunk in range(PEERS // 2):
        rows = slice(16 * chunk, 16 * chunk + 16)
        taps = table_ref[rows, :]
        feat_query = features(q_ref[rows, :].astype(f32), taps[:, 0:3])
        feat_key = features(k_ref[rows, :].astype(f32), taps[:, 3:6])
        feat_value = features(v_ref[rows, :].astype(f32), taps[:, 6:9])
        product = (feat_key * feat_value).astype(bf16).astype(f32)
        finished = lanes_of((16, BLOCK)) < 2
        query_ref[rows, :] = jnp.where(finished, 1.0, taps[:, 9:10] * feat_query)
        skip_ref[rows, :] = jnp.where(finished, 0.0, taps[:, 10:11] * product)


DEPTH = 4
STEPS = 64 // DEPTH


def conv_kernel(msg_ref, aux_ref, out_ref, lag_ref, toep_ref, rows_ref, left_ref, sum_ref):
    lane = lanes_of((256, LANES))
    pad = 8 * (DEPTH - 1)
    edge = jnp.concatenate([msg_ref[place_from(block), TILES].astype(f32) for block in range(PEERS)], axis=0)
    lag_ref[...] = jnp.where(lane < 64, pltpu.roll(edge, 64, 1), pltpu.roll(edge, 255, 0))

    earlier = jnp.concatenate((jnp.zeros((8, LANES), f32), edge[:-8]), axis=0)
    joined = jnp.where(lane % 4 < 2, earlier, edge)

    def spread(index):
        return jnp.concatenate([aux_ref[index]] * PEERS, axis=0)

    feat = (
        spread(0) * joined
        + spread(1) * pltpu.roll(joined, 1, 1)
        + spread(2) * pltpu.roll(joined, 2, 1)
    )
    first_product = pltpu.roll(feat * pltpu.roll(feat, LANES - 4, 1), LANES - 2, 1)
    first_product = first_product.astype(bf16).astype(f32)
    first_query = pltpu.roll(feat, LANES - 10, 1)

    rows_ref[0:pad, :] = jnp.zeros((pad, 256), f32)
    for peer in range(PEERS):
        for tile in range(TILES):
            part = msg_ref[place_from(peer), tile].astype(f32)
            if tile == 0:
                part = jnp.where(lane[:8] < 2, first_product[8 * peer:8 * peer + 8], part)
            start = pad + 16 * peer + 8 * (tile // 2)
            rows_ref[start:start + 8, LANES * (tile % 2):LANES * (tile % 2 + 1)] = part
    for back in range(DEPTH):
        left_ref[:, 256 * back:256 * (back + 1)] = rows_ref[pad - 8 * back:pad - 8 * back + 512, :].astype(bf16)

    lower = lanes_of((LANES, LANES)) >= rows_of((LANES, LANES))
    toep_ref[0] = jnp.zeros((LANES, LANES), bf16)
    turned = jnp.zeros((LANES, LANES), f32)
    for step in range(STEPS):
        for e in range(2 * DEPTH * step, 2 * DEPTH * (step + 1)):
            before = turned
            row = jnp.broadcast_to(lag_ref[2 * e:2 * e + 1, :], (LANES, LANES))
            turned = pltpu.roll(row, 0, 1, stride=1, stride_axis=0)
            toep_ref[e + 1] = jnp.where(lower, turned, before).astype(bf16)
        first = DEPTH * step
        parts = []
        for back in range(DEPTH):
            for half in range(2):
                at = 1 + 2 * (first + back) - half
                parts.append(jnp.concatenate((toep_ref[at], toep_ref[at + 1]), axis=1))
        right = jnp.concatenate(parts, axis=0)
        offset = 8 * first
        got = jnp.dot(left_ref[0:512 - offset, :], right, preferred_element_type=f32)
        if step == 0:
            sum_ref[...] = got
        else:
            sum_ref[offset:, :] += got

        for peer in range(DEPTH // 2 * step, DEPTH // 2 * (step + 1)):
            group = slice(8 * peer, 8 * peer + 8)
            result = sum_ref[16 * peer:16 * peer + 16, :].astype(bf16)
            head = result[0:8, 0:LANES].astype(f32)
            done = aux_ref[3] * first_query[group] * (head + aux_ref[4] * first_product[group])
            out_ref[place_back(peer), :, 0:LANES] = jnp.where(lane[:8] < 2, done, head).astype(bf16)
            out_ref[place_back(peer), :, LANES:256] = result[0:8, LANES:]
            out_ref[place_back(peer), :, 256:512] = result[8:16]


def shards(stream_q, stream_k, stream_v, short_taps, filters, live_mask, skip_gain):
    taps_wide = jnp.transpose(short_taps, (0, 2, 1))
    message = pl.pallas_call(
        message_kernel,
        out_shape=jax.ShapeDtypeStruct((PEERS, TILES + 1, 8, LANES), bf16),
        in_specs=[HBM] * 5,
        out_specs=HBM,
        scratch_shapes=[
            pltpu.VMEM((256, LANES), bf16),
            pltpu.VMEM((256, LANES), bf16),
            pltpu.VMEM((256, BLOCK), bf16),
            pltpu.VMEM((256, BLOCK), bf16),
            pltpu.VMEM((3, 3, 256), f32),
            pltpu.VMEM((16, BLOCK), f32),
            pltpu.VMEM((256, 6 * LANES), f32),
            pltpu.VMEM((PEERS, TILES + 1, 8, LANES), bf16),
            pltpu.SemaphoreType.DMA((6,)),
            pltpu.SemaphoreType.DMA((STORES,)),
        ],
        name="message",
    )(stream_q, stream_k, stream_v, taps_wide, filters)
    arrived = lax.all_to_all(message, "seq", split_axis=0, concat_axis=0, tiled=True, axis_index_groups=[ORDER_OUT])

    query, skip, aux = pl.pallas_call(
        gate_kernel,
        out_shape=[jax.ShapeDtypeStruct((256, BLOCK), f32)] * 2 + [jax.ShapeDtypeStruct((5, OWN, LANES), f32)],
        in_specs=[VMEM] * 6,
        out_specs=[VMEM] * 3,
        scratch_shapes=[pltpu.VMEM((256, 16), f32)],
        compiler_params=pltpu.CompilerParams(vmem_limit_bytes=16 << 20),
        cost_estimate=pl.CostEstimate(flops=4000000, bytes_accessed=2 << 20, transcendentals=0),
        name="gate",
    )(stream_q, stream_k, stream_v, taps_wide, live_mask[None, :], skip_gain[None, :])

    convolved = pl.pallas_call(
        conv_kernel,
        out_shape=jax.ShapeDtypeStruct((PEERS, OWN, BLOCK), bf16),
        in_specs=[VMEM] * 2,
        out_specs=VMEM,
        scratch_shapes=[
            pltpu.VMEM((256, LANES), f32),
            pltpu.VMEM((129, LANES, LANES), bf16),
            pltpu.VMEM((512 + 8 * (DEPTH - 1), 256), f32),
            pltpu.VMEM((512, 256 * DEPTH), bf16),
            pltpu.VMEM((512, 256), f32),
        ],
        compiler_params=pltpu.CompilerParams(vmem_limit_bytes=32 << 20),
        cost_estimate=pl.CostEstimate(flops=2300000000, bytes_accessed=1 << 20, transcendentals=0),
        name="conv",
    )(arrived, aux)
    back = lax.all_to_all(convolved, "seq", split_axis=0, concat_axis=0, tiled=True, axis_index_groups=[ORDER_BACK])
    return (query * (back.reshape(256, BLOCK).astype(f32) + skip)).astype(bf16)


def solution(mesh):
    in_specs = (
        P("tp", "seq"),
        P("tp", "seq"),
        P("tp", "seq"),
        P(None, "tp", None),
        P("tp", "seq"),
        P("tp"),
        P("tp"),
    )
    return jax.shard_map(shards, mesh=mesh, in_specs=in_specs, out_specs=P("tp", "seq"), check_vma=False)
```

```python
import jax
import jax.numpy as jnp
from jax import lax
from jax.experimental import pallas as pl
from jax.experimental.pallas import tpu as pltpu
from jax.sharding import PartitionSpec as P

f32, bf16 = jnp.float32, jnp.bfloat16
PEERS = 32
OWN = 8
BLOCK = 512
LANES = 128
TILES = BLOCK // LANES
FIRST_OUT, FIRST_BACK = 23, 17
IN_TURN = [index for step in range(PEERS // 2) for index in (step, step + PEERS // 2)]
ORDER_OUT = [FIRST_OUT] + [index for index in range(PEERS) if index != FIRST_OUT]
ORDER_BACK = [FIRST_BACK] + [index for index in IN_TURN if index != FIRST_BACK]


def own_group(index):
    half = PEERS // 2
    turn = 2 * lax.rem(index, half) + index // half
    return jnp.where(index == FIRST_BACK, 0, jnp.where(turn < IN_TURN.index(FIRST_BACK), turn + 1, turn))


def place_there(group):
    return ORDER_OUT.index(ORDER_BACK[group])


def place_from(block):
    return ORDER_OUT.index(block)


def place_back(block):
    return ORDER_BACK.index(block)


VMEM = pl.BlockSpec(memory_space=pltpu.VMEM)
HBM = pl.BlockSpec(memory_space=pltpu.HBM)


def lanes_of(shape):
    return lax.broadcasted_iota(jnp.int32, shape, 1)


def rows_of(shape):
    return lax.broadcasted_iota(jnp.int32, shape, 0)


def features(signal, taps):
    return (
        taps[:, 0:1] * signal
        + taps[:, 1:2] * pltpu.roll(signal, 1, 1)
        + taps[:, 2:3] * pltpu.roll(signal, 2, 1)
    )


def columns_of(rows):
    spare = 16 - sum(row.shape[0] for row in rows)
    return jnp.transpose(jnp.concatenate(list(rows) + [jnp.zeros((spare, 256), f32)], axis=0))


def spread_rows(rows):
    count = sum(row.shape[0] for row in rows)
    values = jnp.concatenate(list(rows) + [jnp.zeros((8 - count, 256), f32)], axis=0)
    terms = []
    for _ in range(3):
        terms.append(values.astype(bf16).astype(f32))
        values = values - terms[-1]
    shape = (24, LANES * count)
    pick = (rows_of(shape) % 8 == lanes_of(shape) // LANES).astype(bf16)
    columns = jnp.transpose(jnp.concatenate(terms, axis=0)).astype(bf16)
    return jnp.dot(columns, pick, preferred_element_type=f32)


STORES = 4


def message_kernel(q_hbm, k_hbm, v_hbm, taps_hbm, filt_hbm, out_hbm, qf, ql, kk, vv, taps_ref, filt_ref, wide_ref, out_ref, sems, out_sems):
    loads = [
        pltpu.make_async_copy(taps_hbm, taps_ref, sems.at[0]),
        pltpu.make_async_copy(k_hbm, kk, sems.at[1]),
        pltpu.make_async_copy(v_hbm, vv, sems.at[2]),
        pltpu.make_async_copy(filt_hbm, filt_ref, sems.at[3]),
        pltpu.make_async_copy(q_hbm.at[:, 0:LANES], qf, sems.at[4]),
        pltpu.make_async_copy(q_hbm.at[:, BLOCK - LANES:], ql, sems.at[5]),
    ]
    for copy in loads:
        copy.start()
    loads[0].wait()
    wide_ref[...] = spread_rows((taps_ref[1], taps_ref[2]))
    for copy in loads[1:]:
        copy.wait()
    lane = lanes_of((16, LANES))
    small_row = rows_of((8, LANES))
    group_at = {place_there(group): group for group in range(PEERS)}
    chunks = list(dict.fromkeys(group_at[place] // 2 for place in range(PEERS)))
    stores = []
    for done, chunk in enumerate(chunks):
        rows = slice(16 * chunk, 16 * chunk + 16)
        key = kk[rows, :].astype(f32)
        value = vv[rows, :].astype(f32)

        def features(signal, first):
            taps = [
                jnp.concatenate([wide_ref[rows, LANES * at:LANES * (at + 1)]] * TILES, axis=1)
                for at in range(first, first + 3)
            ]
            return taps[0] * signal + taps[1] * pltpu.roll(signal, 1, 1) + taps[2] * pltpu.roll(signal, 2, 1)

        product = features(key, 0) * features(value, 3)

        def ends(first, last, place):
            return pltpu.roll(jnp.where(lane >= 64, last, first), place, 1)

        k_ends = ends(key[:, 0:LANES], key[:, BLOCK - LANES:], 2)
        v_ends = ends(value[:, 0:LANES], value[:, BLOCK - LANES:], 6)
        q_ends = ends(qf[rows, :].astype(f32), ql[rows, :].astype(f32), 10)
        wide = jnp.where(small_row < 2, filt_ref[chunk:chunk + 1, 0:LANES],
                         jnp.where(small_row < 4, filt_ref[chunk:chunk + 1, LANES:2 * LANES],
                                   jnp.where(small_row < 6, filt_ref[chunk:chunk + 1, 2 * LANES:3 * LANES],
                                             filt_ref[chunk:chunk + 1, 3 * LANES:4 * LANES])))
        lags = jnp.where(small_row % 2 == 1, wide, pltpu.roll(wide, 64, 1))
        lags = jnp.concatenate((lags, lags), axis=0)
        edge = jnp.where(lane < 4, k_ends, jnp.where(lane < 8, v_ends, jnp.where(lane < 12, q_ends, lags)))
        for half in range(2):
            place = place_there(2 * chunk + half)
            piece = slice(8 * half, 8 * half + 8)
            for tile in range(TILES):
                out_ref[place, tile] = product[piece, LANES * tile:LANES * (tile + 1)].astype(bf16)
            out_ref[place, TILES] = edge[piece].astype(bf16)
        full = {place_there(2 * chunk + half) for chunk in chunks[:done + 1] for half in range(2)}
        while len(stores) < STORES:
            span = slice(PEERS // STORES * len(stores), PEERS // STORES * (len(stores) + 1))
            if not full.issuperset(range(span.start, span.stop)):
                break
            stores.append(pltpu.make_async_copy(out_ref.at[span], out_hbm.at[span], out_sems.at[len(stores)]))
            stores[-1].start()
    assert len(stores) == STORES
    for copy in stores:
        copy.wait()


def gate_kernel(q_ref, k_ref, v_ref, taps_ref, live_ref, gain_ref, query_ref, skip_ref, aux_ref, table_ref):
    table_ref[...] = columns_of(
        (taps_ref[0], taps_ref[1], taps_ref[2], live_ref[...].astype(f32), gain_ref[...])
    )
    own = table_ref[pl.ds(pl.multiple_of(own_group(lax.axis_index("seq")) * OWN, OWN), OWN), :]
    kind = lanes_of((OWN, LANES)) // 4
    for tap in range(3):
        aux_ref[tap] = jnp.where(
            kind == 0, own[:, 3 + tap:4 + tap], jnp.where(kind == 1, own[:, 6 + tap:7 + tap], own[:, tap:tap + 1])
        )
    for place in range(2):
        aux_ref[3 + place] = jnp.broadcast_to(own[:, 9 + place:10 + place], (OWN, LANES))
    for chunk in range(PEERS // 2):
        rows = slice(16 * chunk, 16 * chunk + 16)
        taps = table_ref[rows, :]
        feat_query = features(q_ref[rows, :].astype(f32), taps[:, 0:3])
        feat_key = features(k_ref[rows, :].astype(f32), taps[:, 3:6])
        feat_value = features(v_ref[rows, :].astype(f32), taps[:, 6:9])
        product = (feat_key * feat_value).astype(bf16).astype(f32)
        finished = lanes_of((16, BLOCK)) < 2
        query_ref[rows, :] = jnp.where(finished, 1.0, taps[:, 9:10] * feat_query)
        skip_ref[rows, :] = jnp.where(finished, 0.0, taps[:, 10:11] * product)


def final_kernel(back_ref, query_ref, skip_ref, out_hbm, out_ref, sems):
    parts = sems.shape[0]
    copies = []
    for part in range(parts):
        groups = slice(PEERS // parts * part, PEERS // parts * (part + 1))
        rows = slice(OWN * groups.start, OWN * groups.stop)
        back = back_ref[groups].astype(f32).reshape(OWN * PEERS // parts, BLOCK)
        out_ref[rows, :] = (query_ref[rows, :] * (back + skip_ref[rows, :])).astype(bf16)
        copies.append(pltpu.make_async_copy(out_ref.at[rows], out_hbm.at[rows], sems.at[part]))
        copies[-1].start()
    for copy in copies:
        copy.wait()


DEPTH = 4
STEPS = 64 // DEPTH


def conv_kernel(msg_ref, aux_ref, out_ref, lag_ref, toep_ref, rows_ref, left_ref, sum_ref):
    lane = lanes_of((256, LANES))
    pad = 8 * (DEPTH - 1)
    edge = jnp.concatenate([msg_ref[place_from(block), TILES].astype(f32) for block in range(PEERS)], axis=0)
    lag_ref[...] = jnp.where(lane < 64, pltpu.roll(edge, 64, 1), pltpu.roll(edge, 255, 0))

    earlier = jnp.concatenate((jnp.zeros((8, LANES), f32), edge[:-8]), axis=0)
    joined = jnp.where(lane % 4 < 2, earlier, edge)

    def spread(index):
        return jnp.concatenate([aux_ref[index]] * PEERS, axis=0)

    feat = (
        spread(0) * joined
        + spread(1) * pltpu.roll(joined, 1, 1)
        + spread(2) * pltpu.roll(joined, 2, 1)
    )
    first_product = pltpu.roll(feat * pltpu.roll(feat, LANES - 4, 1), LANES - 2, 1)
    first_product = first_product.astype(bf16).astype(f32)
    first_query = pltpu.roll(feat, LANES - 10, 1)

    rows_ref[0:pad, :] = jnp.zeros((pad, 256), f32)
    for peer in range(PEERS):
        for tile in range(TILES):
            part = msg_ref[place_from(peer), tile].astype(f32)
            if tile == 0:
                part = jnp.where(lane[:8] < 2, first_product[8 * peer:8 * peer + 8], part)
            start = pad + 16 * peer + 8 * (tile // 2)
            rows_ref[start:start + 8, LANES * (tile % 2):LANES * (tile % 2 + 1)] = part
    for back in range(DEPTH):
        left_ref[:, 256 * back:256 * (back + 1)] = rows_ref[pad - 8 * back:pad - 8 * back + 512, :].astype(bf16)

    lower = lanes_of((LANES, LANES)) >= rows_of((LANES, LANES))
    toep_ref[0] = jnp.zeros((LANES, LANES), bf16)
    turned = jnp.zeros((LANES, LANES), f32)
    for step in range(STEPS):
        for e in range(2 * DEPTH * step, 2 * DEPTH * (step + 1)):
            before = turned
            row = jnp.broadcast_to(lag_ref[2 * e:2 * e + 1, :], (LANES, LANES))
            turned = pltpu.roll(row, 0, 1, stride=1, stride_axis=0)
            toep_ref[e + 1] = jnp.where(lower, turned, before).astype(bf16)
        first = DEPTH * step
        parts = []
        for back in range(DEPTH):
            for half in range(2):
                at = 1 + 2 * (first + back) - half
                parts.append(jnp.concatenate((toep_ref[at], toep_ref[at + 1]), axis=1))
        right = jnp.concatenate(parts, axis=0)
        offset = 8 * first
        got = jnp.dot(left_ref[0:512 - offset, :], right, preferred_element_type=f32)
        if step == 0:
            sum_ref[...] = got
        else:
            sum_ref[offset:, :] += got

        for peer in range(DEPTH // 2 * step, DEPTH // 2 * (step + 1)):
            group = slice(8 * peer, 8 * peer + 8)
            result = sum_ref[16 * peer:16 * peer + 16, :].astype(bf16)
            head = result[0:8, 0:LANES].astype(f32)
            done = aux_ref[3] * first_query[group] * (head + aux_ref[4] * first_product[group])
            out_ref[place_back(peer), :, 0:LANES] = jnp.where(lane[:8] < 2, done, head).astype(bf16)
            out_ref[place_back(peer), :, LANES:256] = result[0:8, LANES:]
            out_ref[place_back(peer), :, 256:512] = result[8:16]


def shards(stream_q, stream_k, stream_v, short_taps, filters, live_mask, skip_gain):
    taps_wide = jnp.transpose(short_taps, (0, 2, 1))
    message = pl.pallas_call(
        message_kernel,
        out_shape=jax.ShapeDtypeStruct((PEERS, TILES + 1, 8, LANES), bf16),
        in_specs=[HBM] * 5,
        out_specs=HBM,
        scratch_shapes=[
            pltpu.VMEM((256, LANES), bf16),
            pltpu.VMEM((256, LANES), bf16),
            pltpu.VMEM((256, BLOCK), bf16),
            pltpu.VMEM((256, BLOCK), bf16),
            pltpu.VMEM((3, 3, 256), f32),
            pltpu.VMEM((16, BLOCK), f32),
            pltpu.VMEM((256, 6 * LANES), f32),
            pltpu.VMEM((PEERS, TILES + 1, 8, LANES), bf16),
            pltpu.SemaphoreType.DMA((6,)),
            pltpu.SemaphoreType.DMA((STORES,)),
        ],
        name="message",
    )(stream_q, stream_k, stream_v, taps_wide, filters)
    arrived = lax.all_to_all(message, "seq", split_axis=0, concat_axis=0, tiled=True, axis_index_groups=[ORDER_OUT])

    query, skip, aux = pl.pallas_call(
        gate_kernel,
        out_shape=[jax.ShapeDtypeStruct((256, BLOCK), f32)] * 2 + [jax.ShapeDtypeStruct((5, OWN, LANES), f32)],
        in_specs=[VMEM] * 6,
        out_specs=[VMEM] * 3,
        scratch_shapes=[pltpu.VMEM((256, 16), f32)],
        compiler_params=pltpu.CompilerParams(vmem_limit_bytes=16 << 20),
        cost_estimate=pl.CostEstimate(flops=4000000, bytes_accessed=2 << 20, transcendentals=0),
        name="gate",
    )(stream_q, stream_k, stream_v, taps_wide, live_mask[None, :], skip_gain[None, :])

    convolved = pl.pallas_call(
        conv_kernel,
        out_shape=jax.ShapeDtypeStruct((PEERS, OWN, BLOCK), bf16),
        in_specs=[VMEM] * 2,
        out_specs=VMEM,
        scratch_shapes=[
            pltpu.VMEM((256, LANES), f32),
            pltpu.VMEM((129, LANES, LANES), bf16),
            pltpu.VMEM((512 + 8 * (DEPTH - 1), 256), f32),
            pltpu.VMEM((512, 256 * DEPTH), bf16),
            pltpu.VMEM((512, 256), f32),
        ],
        compiler_params=pltpu.CompilerParams(vmem_limit_bytes=32 << 20),
        cost_estimate=pl.CostEstimate(flops=2300000000, bytes_accessed=1 << 20, transcendentals=0),
        name="conv",
    )(arrived, aux)
    back = lax.all_to_all(convolved, "seq", split_axis=0, concat_axis=0, tiled=True, axis_index_groups=[ORDER_BACK])
    return pl.pallas_call(
        final_kernel,
        out_shape=jax.ShapeDtypeStruct((256, BLOCK), bf16),
        in_specs=[VMEM] * 3,
        out_specs=HBM,
        scratch_shapes=[pltpu.VMEM((256, BLOCK), bf16), pltpu.SemaphoreType.DMA((4,))],
        compiler_params=pltpu.CompilerParams(vmem_limit_bytes=16 << 20),
        name="final",
    )(back, query, skip)


def solution(mesh):
    in_specs = (
        P("tp", "seq"),
        P("tp", "seq"),
        P("tp", "seq"),
        P(None, "tp", None),
        P("tp", "seq"),
        P("tp"),
        P("tp"),
    )
    return jax.shard_map(shards, mesh=mesh, in_specs=in_specs, out_specs=P("tp", "seq"), check_vma=False)
```

```python
import jax
import jax.numpy as jnp
from jax import lax
from jax.experimental import pallas as pl
from jax.experimental.pallas import tpu as pltpu
from jax.sharding import PartitionSpec as P

f32, bf16 = jnp.float32, jnp.bfloat16
PEERS = 32
OWN = 8
BLOCK = 512
LANES = 128
TILES = BLOCK // LANES
FIRST_BACK = 17
IN_TURN = [index for step in range(PEERS // 2) for index in (step, step + PEERS // 2)]
ORDER_OUT = [
    23, 26, 17, 11, 10, 28, 1, 5, 4, 7, 16, 9, 19, 30, 13, 22,
    0, 21, 29, 6, 12, 20, 14, 15, 3, 31, 2, 24, 25, 27, 18, 8,
]
ORDER_BACK = [FIRST_BACK] + [index for index in IN_TURN if index != FIRST_BACK]


def own_group(index):
    half = PEERS // 2
    turn = 2 * lax.rem(index, half) + index // half
    return jnp.where(index == FIRST_BACK, 0, jnp.where(turn < IN_TURN.index(FIRST_BACK), turn + 1, turn))


def place_there(group):
    return ORDER_OUT.index(ORDER_BACK[group])


def place_from(block):
    return ORDER_OUT.index(block)


def place_back(block):
    return ORDER_BACK.index(block)


VMEM = pl.BlockSpec(memory_space=pltpu.VMEM)
HBM = pl.BlockSpec(memory_space=pltpu.HBM)


def lanes_of(shape):
    return lax.broadcasted_iota(jnp.int32, shape, 1)


def rows_of(shape):
    return lax.broadcasted_iota(jnp.int32, shape, 0)


def features(signal, taps):
    return (
        taps[:, 0:1] * signal
        + taps[:, 1:2] * pltpu.roll(signal, 1, 1)
        + taps[:, 2:3] * pltpu.roll(signal, 2, 1)
    )


def columns_of(rows):
    spare = 16 - sum(row.shape[0] for row in rows)
    return jnp.transpose(jnp.concatenate(list(rows) + [jnp.zeros((spare, 256), f32)], axis=0))


def spread_rows(rows):
    count = sum(row.shape[0] for row in rows)
    values = jnp.concatenate(list(rows) + [jnp.zeros((8 - count, 256), f32)], axis=0)
    terms = []
    for _ in range(3):
        terms.append(values.astype(bf16).astype(f32))
        values = values - terms[-1]
    shape = (24, LANES * count)
    pick = (rows_of(shape) % 8 == lanes_of(shape) // LANES).astype(bf16)
    columns = jnp.transpose(jnp.concatenate(terms, axis=0)).astype(bf16)
    return jnp.dot(columns, pick, preferred_element_type=f32)


STORES = 4


def message_kernel(q_hbm, k_hbm, v_hbm, taps_hbm, filt_hbm, out_hbm, qf, ql, kk, vv, taps_ref, filt_ref, wide_ref, out_ref, sems, out_sems):
    loads = [
        pltpu.make_async_copy(taps_hbm, taps_ref, sems.at[0]),
        pltpu.make_async_copy(k_hbm, kk, sems.at[1]),
        pltpu.make_async_copy(v_hbm, vv, sems.at[2]),
        pltpu.make_async_copy(filt_hbm, filt_ref, sems.at[3]),
        pltpu.make_async_copy(q_hbm.at[:, 0:LANES], qf, sems.at[4]),
        pltpu.make_async_copy(q_hbm.at[:, BLOCK - LANES:], ql, sems.at[5]),
    ]
    for copy in loads:
        copy.start()
    loads[0].wait()
    wide_ref[...] = spread_rows((taps_ref[1], taps_ref[2]))
    for copy in loads[1:]:
        copy.wait()
    lane = lanes_of((16, LANES))
    small_row = rows_of((8, LANES))
    group_at = {place_there(group): group for group in range(PEERS)}
    chunks = list(dict.fromkeys(group_at[place] // 2 for place in range(PEERS)))
    stores = []
    for done, chunk in enumerate(chunks):
        rows = slice(16 * chunk, 16 * chunk + 16)
        key = kk[rows, :].astype(f32)
        value = vv[rows, :].astype(f32)

        def features(signal, first):
            taps = [
                jnp.concatenate([wide_ref[rows, LANES * at:LANES * (at + 1)]] * TILES, axis=1)
                for at in range(first, first + 3)
            ]
            return taps[0] * signal + taps[1] * pltpu.roll(signal, 1, 1) + taps[2] * pltpu.roll(signal, 2, 1)

        product = features(key, 0) * features(value, 3)

        def ends(first, last, place):
            return pltpu.roll(jnp.where(lane >= 64, last, first), place, 1)

        k_ends = ends(key[:, 0:LANES], key[:, BLOCK - LANES:], 2)
        v_ends = ends(value[:, 0:LANES], value[:, BLOCK - LANES:], 6)
        q_ends = ends(qf[rows, :].astype(f32), ql[rows, :].astype(f32), 10)
        wide = jnp.where(small_row < 2, filt_ref[chunk:chunk + 1, 0:LANES],
                         jnp.where(small_row < 4, filt_ref[chunk:chunk + 1, LANES:2 * LANES],
                                   jnp.where(small_row < 6, filt_ref[chunk:chunk + 1, 2 * LANES:3 * LANES],
                                             filt_ref[chunk:chunk + 1, 3 * LANES:4 * LANES])))
        lags = jnp.where(small_row % 2 == 1, wide, pltpu.roll(wide, 64, 1))
        lags = jnp.concatenate((lags, lags), axis=0)
        edge = jnp.where(lane < 4, k_ends, jnp.where(lane < 8, v_ends, jnp.where(lane < 12, q_ends, lags)))
        for half in range(2):
            place = place_there(2 * chunk + half)
            piece = slice(8 * half, 8 * half + 8)
            for tile in range(TILES):
                out_ref[place, tile] = product[piece, LANES * tile:LANES * (tile + 1)].astype(bf16)
            out_ref[place, TILES] = edge[piece].astype(bf16)
        full = {place_there(2 * chunk + half) for chunk in chunks[:done + 1] for half in range(2)}
        while len(stores) < STORES:
            span = slice(PEERS // STORES * len(stores), PEERS // STORES * (len(stores) + 1))
            if not full.issuperset(range(span.start, span.stop)):
                break
            stores.append(pltpu.make_async_copy(out_ref.at[span], out_hbm.at[span], out_sems.at[len(stores)]))
            stores[-1].start()
    assert len(stores) == STORES
    for copy in stores:
        copy.wait()


def gate_kernel(q_ref, k_ref, v_ref, taps_ref, live_ref, gain_ref, query_ref, skip_ref, aux_ref, table_ref):
    table_ref[...] = columns_of(
        (taps_ref[0], taps_ref[1], taps_ref[2], live_ref[...].astype(f32), gain_ref[...])
    )
    own = table_ref[pl.ds(pl.multiple_of(own_group(lax.axis_index("seq")) * OWN, OWN), OWN), :]
    kind = lanes_of((OWN, LANES)) // 4
    for tap in range(3):
        aux_ref[tap] = jnp.where(
            kind == 0, own[:, 3 + tap:4 + tap], jnp.where(kind == 1, own[:, 6 + tap:7 + tap], own[:, tap:tap + 1])
        )
    for place in range(2):
        aux_ref[3 + place] = jnp.broadcast_to(own[:, 9 + place:10 + place], (OWN, LANES))
    for chunk in range(PEERS // 2):
        rows = slice(16 * chunk, 16 * chunk + 16)
        taps = table_ref[rows, :]
        feat_query = features(q_ref[rows, :].astype(f32), taps[:, 0:3])
        feat_key = features(k_ref[rows, :].astype(f32), taps[:, 3:6])
        feat_value = features(v_ref[rows, :].astype(f32), taps[:, 6:9])
        product = (feat_key * feat_value).astype(bf16).astype(f32)
        finished = lanes_of((16, BLOCK)) < 2
        query_ref[rows, :] = jnp.where(finished, 1.0, taps[:, 9:10] * feat_query)
        skip_ref[rows, :] = jnp.where(finished, 0.0, taps[:, 10:11] * product)


def final_kernel(back_ref, query_ref, skip_ref, out_hbm, out_ref, sems):
    parts = sems.shape[0]
    copies = []
    for part in range(parts):
        groups = slice(PEERS // parts * part, PEERS // parts * (part + 1))
        rows = slice(OWN * groups.start, OWN * groups.stop)
        back = back_ref[groups].astype(f32).reshape(OWN * PEERS // parts, BLOCK)
        out_ref[rows, :] = (query_ref[rows, :] * (back + skip_ref[rows, :])).astype(bf16)
        copies.append(pltpu.make_async_copy(out_ref.at[rows], out_hbm.at[rows], sems.at[part]))
        copies[-1].start()
    for copy in copies:
        copy.wait()


DEPTH = 4
STEPS = 64 // DEPTH
TAIL = 12


def conv_kernel(msg_ref, aux_ref, out_ref, lag_ref, toep_ref, rows_ref, left_ref, sum_ref):
    lane = lanes_of((256, LANES))
    pad = 8 * (DEPTH - 1)
    edge = jnp.concatenate([msg_ref[place_from(block), TILES].astype(f32) for block in range(PEERS)], axis=0)
    lag_ref[...] = jnp.where(lane < 64, pltpu.roll(edge, 64, 1), pltpu.roll(edge, 255, 0))

    earlier = jnp.concatenate((jnp.zeros((8, LANES), f32), edge[:-8]), axis=0)
    joined = jnp.where(lane % 4 < 2, earlier, edge)

    def spread(index):
        return jnp.concatenate([aux_ref[index]] * PEERS, axis=0)

    feat = (
        spread(0) * joined
        + spread(1) * pltpu.roll(joined, 1, 1)
        + spread(2) * pltpu.roll(joined, 2, 1)
    )
    first_product = pltpu.roll(feat * pltpu.roll(feat, LANES - 4, 1), LANES - 2, 1)
    first_product = first_product.astype(bf16).astype(f32)
    first_query = pltpu.roll(feat, LANES - 10, 1)

    rows_ref[0:pad, :] = jnp.zeros((pad, 256), f32)
    for peer in range(PEERS):
        for tile in range(TILES):
            part = msg_ref[place_from(peer), tile].astype(f32)
            if tile == 0:
                part = jnp.where(lane[:8] < 2, first_product[8 * peer:8 * peer + 8], part)
            start = pad + 16 * peer + 8 * (tile // 2)
            rows_ref[start:start + 8, LANES * (tile % 2):LANES * (tile % 2 + 1)] = part
    for back in range(DEPTH):
        left_ref[:, 256 * back:256 * (back + 1)] = rows_ref[pad - 8 * back:pad - 8 * back + 512, :].astype(bf16)

    lower = lanes_of((LANES, LANES)) >= rows_of((LANES, LANES))
    toep_ref[0] = jnp.zeros((LANES, LANES), bf16)
    turned = jnp.zeros((LANES, LANES), f32)
    for step in range(STEPS):
        for e in range(2 * DEPTH * step, 2 * DEPTH * (step + 1)):
            before = turned
            row = jnp.broadcast_to(lag_ref[2 * e:2 * e + 1, :], (LANES, LANES))
            turned = pltpu.roll(row, 0, 1, stride=1, stride_axis=0)
            toep_ref[e + 1] = jnp.where(lower, turned, before).astype(bf16)
        if TAIL <= step < STEPS - 1:
            continue
        head = TAIL if step == STEPS - 1 else step
        offset = 8 * DEPTH * head
        lefts, parts = [], []
        for part in range(head, step + 1):
            gap = 8 * DEPTH * (part - head)
            left = left_ref[0:512 - offset - gap, :]
            if gap:
                left = jnp.concatenate((jnp.zeros((gap, 256 * DEPTH), bf16), left), axis=0)
            lefts.append(left)
            for back in range(DEPTH):
                for half in range(2):
                    at = 1 + 2 * (DEPTH * part + back) - half
                    parts.append(jnp.concatenate((toep_ref[at], toep_ref[at + 1]), axis=1))
        right = jnp.concatenate(parts, axis=0)
        got = jnp.dot(jnp.concatenate(lefts, axis=1), right, preferred_element_type=f32)
        if step == 0:
            sum_ref[...] = got
        else:
            sum_ref[offset:, :] += got

        for peer in range(DEPTH // 2 * head, DEPTH // 2 * (step + 1)):
            group = slice(8 * peer, 8 * peer + 8)
            result = sum_ref[16 * peer:16 * peer + 16, :].astype(bf16)
            head = result[0:8, 0:LANES].astype(f32)
            done = aux_ref[3] * first_query[group] * (head + aux_ref[4] * first_product[group])
            out_ref[place_back(peer), :, 0:LANES] = jnp.where(lane[:8] < 2, done, head).astype(bf16)
            out_ref[place_back(peer), :, LANES:256] = result[0:8, LANES:]
            out_ref[place_back(peer), :, 256:512] = result[8:16]


def shards(stream_q, stream_k, stream_v, short_taps, filters, live_mask, skip_gain):
    taps_wide = jnp.transpose(short_taps, (0, 2, 1))
    message = pl.pallas_call(
        message_kernel,
        out_shape=jax.ShapeDtypeStruct((PEERS, TILES + 1, 8, LANES), bf16),
        in_specs=[HBM] * 5,
        out_specs=HBM,
        scratch_shapes=[
            pltpu.VMEM((256, LANES), bf16),
            pltpu.VMEM((256, LANES), bf16),
            pltpu.VMEM((256, BLOCK), bf16),
            pltpu.VMEM((256, BLOCK), bf16),
            pltpu.VMEM((3, 3, 256), f32),
            pltpu.VMEM((16, BLOCK), f32),
            pltpu.VMEM((256, 6 * LANES), f32),
            pltpu.VMEM((PEERS, TILES + 1, 8, LANES), bf16),
            pltpu.SemaphoreType.DMA((6,)),
            pltpu.SemaphoreType.DMA((STORES,)),
        ],
        name="message",
    )(stream_q, stream_k, stream_v, taps_wide, filters)
    arrived = lax.all_to_all(message, "seq", split_axis=0, concat_axis=0, tiled=True, axis_index_groups=[ORDER_OUT])

    query, skip, aux = pl.pallas_call(
        gate_kernel,
        out_shape=[jax.ShapeDtypeStruct((256, BLOCK), f32)] * 2 + [jax.ShapeDtypeStruct((5, OWN, LANES), f32)],
        in_specs=[VMEM] * 6,
        out_specs=[VMEM] * 3,
        scratch_shapes=[pltpu.VMEM((256, 16), f32)],
        compiler_params=pltpu.CompilerParams(vmem_limit_bytes=16 << 20),
        cost_estimate=pl.CostEstimate(flops=4000000, bytes_accessed=2 << 20, transcendentals=0),
        name="gate",
    )(stream_q, stream_k, stream_v, taps_wide, live_mask[None, :], skip_gain[None, :])

    convolved = pl.pallas_call(
        conv_kernel,
        out_shape=jax.ShapeDtypeStruct((PEERS, OWN, BLOCK), bf16),
        in_specs=[VMEM] * 2,
        out_specs=VMEM,
        scratch_shapes=[
            pltpu.VMEM((256, LANES), f32),
            pltpu.VMEM((129, LANES, LANES), bf16),
            pltpu.VMEM((512 + 8 * (DEPTH - 1), 256), f32),
            pltpu.VMEM((512, 256 * DEPTH), bf16),
            pltpu.VMEM((512, 256), f32),
        ],
        compiler_params=pltpu.CompilerParams(vmem_limit_bytes=32 << 20),
        cost_estimate=pl.CostEstimate(flops=2300000000, bytes_accessed=1 << 20, transcendentals=0),
        name="conv",
    )(arrived, aux)
    back = lax.all_to_all(convolved, "seq", split_axis=0, concat_axis=0, tiled=True, axis_index_groups=[ORDER_BACK])
    return pl.pallas_call(
        final_kernel,
        out_shape=jax.ShapeDtypeStruct((256, BLOCK), bf16),
        in_specs=[VMEM] * 3,
        out_specs=HBM,
        scratch_shapes=[pltpu.VMEM((256, BLOCK), bf16), pltpu.SemaphoreType.DMA((4,))],
        compiler_params=pltpu.CompilerParams(vmem_limit_bytes=16 << 20),
        name="final",
    )(back, query, skip)


def solution(mesh):
    in_specs = (
        P("tp", "seq"),
        P("tp", "seq"),
        P("tp", "seq"),
        P(None, "tp", None),
        P("tp", "seq"),
        P("tp"),
        P("tp"),
    )
    return jax.shard_map(shards, mesh=mesh, in_specs=in_specs, out_specs=P("tp", "seq"), check_vma=False)
```

```python
import jax
import jax.numpy as jnp
from jax import lax
from jax.experimental import pallas as pl
from jax.experimental.pallas import tpu as pltpu
from jax.sharding import PartitionSpec as P

f32, bf16 = jnp.float32, jnp.bfloat16
PEERS = 32
OWN = 8
BLOCK = 512
LANES = 128
TILES = BLOCK // LANES
FIRST_BACK = 17
IN_TURN = [index for step in range(PEERS // 2) for index in (step, step + PEERS // 2)]
ORDER_OUT = [
    23, 26, 17, 11, 10, 28, 1, 5, 4, 7, 16, 9, 19, 30, 13, 22,
    0, 21, 29, 6, 12, 20, 14, 15, 3, 31, 2, 24, 25, 27, 18, 8,
]
ORDER_BACK = [FIRST_BACK] + [index for index in IN_TURN if index != FIRST_BACK]


def own_group(index):
    half = PEERS // 2
    turn = 2 * lax.rem(index, half) + index // half
    return jnp.where(index == FIRST_BACK, 0, jnp.where(turn < IN_TURN.index(FIRST_BACK), turn + 1, turn))


def place_there(group):
    return ORDER_OUT.index(ORDER_BACK[group])


def place_from(block):
    return ORDER_OUT.index(block)


def place_back(block):
    return ORDER_BACK.index(block)


VMEM = pl.BlockSpec(memory_space=pltpu.VMEM)
HBM = pl.BlockSpec(memory_space=pltpu.HBM)


def lanes_of(shape):
    return lax.broadcasted_iota(jnp.int32, shape, 1)


def rows_of(shape):
    return lax.broadcasted_iota(jnp.int32, shape, 0)


def features(signal, taps):
    return (
        taps[:, 0:1] * signal
        + taps[:, 1:2] * pltpu.roll(signal, 1, 1)
        + taps[:, 2:3] * pltpu.roll(signal, 2, 1)
    )


def columns_of(rows):
    spare = 16 - sum(row.shape[0] for row in rows)
    return jnp.transpose(jnp.concatenate(list(rows) + [jnp.zeros((spare, 256), f32)], axis=0))


def spread_rows(rows):
    count = sum(row.shape[0] for row in rows)
    values = jnp.concatenate(list(rows) + [jnp.zeros((8 - count, 256), f32)], axis=0)
    terms = []
    for _ in range(3):
        terms.append(values.astype(bf16).astype(f32))
        values = values - terms[-1]
    shape = (24, LANES * count)
    pick = (rows_of(shape) % 8 == lanes_of(shape) // LANES).astype(bf16)
    columns = jnp.transpose(jnp.concatenate(terms, axis=0)).astype(bf16)
    return jnp.dot(columns, pick, preferred_element_type=f32)


STORES = 4


def message_kernel(q_hbm, k_hbm, v_hbm, taps_hbm, filt_hbm, out_hbm, qf, ql, kk, vv, taps_ref, filt_ref, wide_ref, out_ref, sems, out_sems):
    loads = [
        pltpu.make_async_copy(taps_hbm, taps_ref, sems.at[0]),
        pltpu.make_async_copy(k_hbm, kk, sems.at[1]),
        pltpu.make_async_copy(v_hbm, vv, sems.at[2]),
        pltpu.make_async_copy(filt_hbm, filt_ref, sems.at[3]),
        pltpu.make_async_copy(q_hbm.at[:, 0:LANES], qf, sems.at[4]),
        pltpu.make_async_copy(q_hbm.at[:, BLOCK - LANES:], ql, sems.at[5]),
    ]
    for copy in loads:
        copy.start()
    loads[0].wait()
    wide_ref[...] = spread_rows((taps_ref[1], taps_ref[2]))
    for copy in loads[1:]:
        copy.wait()
    lane = lanes_of((16, LANES))
    small_row = rows_of((8, LANES))
    group_at = {place_there(group): group for group in range(PEERS)}
    chunks = list(dict.fromkeys(group_at[place] // 2 for place in range(PEERS)))
    stores = []
    for done, chunk in enumerate(chunks):
        rows = slice(16 * chunk, 16 * chunk + 16)
        key = kk[rows, :].astype(f32)
        value = vv[rows, :].astype(f32)

        def features(signal, first):
            taps = [
                jnp.concatenate([wide_ref[rows, LANES * at:LANES * (at + 1)]] * TILES, axis=1)
                for at in range(first, first + 3)
            ]
            return taps[0] * signal + taps[1] * pltpu.roll(signal, 1, 1) + taps[2] * pltpu.roll(signal, 2, 1)

        product = features(key, 0) * features(value, 3)

        def ends(first, last, place):
            return pltpu.roll(jnp.where(lane >= 64, last, first), place, 1)

        k_ends = ends(key[:, 0:LANES], key[:, BLOCK - LANES:], 2)
        v_ends = ends(value[:, 0:LANES], value[:, BLOCK - LANES:], 6)
        q_ends = ends(qf[rows, :].astype(f32), ql[rows, :].astype(f32), 10)
        wide = jnp.where(small_row < 2, filt_ref[chunk:chunk + 1, 0:LANES],
                         jnp.where(small_row < 4, filt_ref[chunk:chunk + 1, LANES:2 * LANES],
                                   jnp.where(small_row < 6, filt_ref[chunk:chunk + 1, 2 * LANES:3 * LANES],
                                             filt_ref[chunk:chunk + 1, 3 * LANES:4 * LANES])))
        lags = jnp.where(small_row % 2 == 1, wide, pltpu.roll(wide, 64, 1))
        lags = jnp.concatenate((lags, lags), axis=0)
        edge = jnp.where(lane < 4, k_ends, jnp.where(lane < 8, v_ends, jnp.where(lane < 12, q_ends, lags)))
        for half in range(2):
            place = place_there(2 * chunk + half)
            piece = slice(8 * half, 8 * half + 8)
            for tile in range(TILES):
                out_ref[place, tile] = product[piece, LANES * tile:LANES * (tile + 1)].astype(bf16)
            out_ref[place, TILES] = edge[piece].astype(bf16)
        full = {place_there(2 * chunk + half) for chunk in chunks[:done + 1] for half in range(2)}
        while len(stores) < STORES:
            span = slice(PEERS // STORES * len(stores), PEERS // STORES * (len(stores) + 1))
            if not full.issuperset(range(span.start, span.stop)):
                break
            stores.append(pltpu.make_async_copy(out_ref.at[span], out_hbm.at[span], out_sems.at[len(stores)]))
            stores[-1].start()
    assert len(stores) == STORES
    for copy in stores:
        copy.wait()


def gate_kernel(q_ref, k_ref, v_ref, taps_ref, live_ref, gain_ref, query_ref, skip_ref, aux_ref, table_ref):
    table_ref[...] = columns_of(
        (taps_ref[0], taps_ref[1], taps_ref[2], live_ref[...].astype(f32), gain_ref[...])
    )
    own = table_ref[pl.ds(pl.multiple_of(own_group(lax.axis_index("seq")) * OWN, OWN), OWN), :]
    kind = lanes_of((OWN, LANES)) // 4
    for tap in range(3):
        aux_ref[tap] = jnp.where(
            kind == 0, own[:, 3 + tap:4 + tap], jnp.where(kind == 1, own[:, 6 + tap:7 + tap], own[:, tap:tap + 1])
        )
    for place in range(2):
        aux_ref[3 + place] = jnp.broadcast_to(own[:, 9 + place:10 + place], (OWN, LANES))
    for chunk in range(PEERS // 2):
        rows = slice(16 * chunk, 16 * chunk + 16)
        taps = table_ref[rows, :]
        feat_query = features(q_ref[rows, :].astype(f32), taps[:, 0:3])
        feat_key = features(k_ref[rows, :].astype(f32), taps[:, 3:6])
        feat_value = features(v_ref[rows, :].astype(f32), taps[:, 6:9])
        product = (feat_key * feat_value).astype(bf16).astype(f32)
        finished = lanes_of((16, BLOCK)) < 2
        query_ref[rows, :] = jnp.where(finished, 1.0, taps[:, 9:10] * feat_query)
        skip_ref[rows, :] = jnp.where(finished, 0.0, taps[:, 10:11] * product)


def final_kernel(back_ref, query_ref, skip_ref, out_hbm, out_ref, sems):
    parts = sems.shape[0]
    copies = []
    for part in range(parts):
        groups = slice(PEERS // parts * part, PEERS // parts * (part + 1))
        rows = slice(OWN * groups.start, OWN * groups.stop)
        back = back_ref[groups].astype(f32).reshape(OWN * PEERS // parts, BLOCK)
        out_ref[rows, :] = (query_ref[rows, :] * (back + skip_ref[rows, :])).astype(bf16)
        copies.append(pltpu.make_async_copy(out_ref.at[rows], out_hbm.at[rows], sems.at[part]))
        copies[-1].start()
    for copy in copies:
        copy.wait()


DEPTH = 4
STEPS = 64 // DEPTH
TAIL = 12


def conv_kernel(msg_ref, aux_ref, out_ref, lag_ref, toep_ref, rows_ref, left_ref, sum_ref):
    lane = lanes_of((256, LANES))
    pad = 8 * (DEPTH - 1)
    edge = jnp.concatenate([msg_ref[place_from(block), TILES].astype(f32) for block in range(PEERS)], axis=0)
    lag_ref[...] = jnp.where(lane < 64, pltpu.roll(edge, 64, 1), pltpu.roll(edge, 255, 0))

    earlier = jnp.concatenate((jnp.zeros((8, LANES), f32), edge[:-8]), axis=0)
    joined = jnp.where(lane % 4 < 2, earlier, edge)

    def spread(index):
        return jnp.concatenate([aux_ref[index]] * PEERS, axis=0)

    feat = (
        spread(0) * joined
        + spread(1) * pltpu.roll(joined, 1, 1)
        + spread(2) * pltpu.roll(joined, 2, 1)
    )
    first_product = pltpu.roll(feat * pltpu.roll(feat, LANES - 4, 1), LANES - 2, 1)
    first_product = first_product.astype(bf16).astype(f32)
    first_query = pltpu.roll(feat, LANES - 10, 1)

    rows_ref[0:pad, :] = jnp.zeros((pad, 256), f32)
    for peer in range(PEERS):
        for tile in range(TILES):
            part = msg_ref[place_from(peer), tile].astype(f32)
            if tile == 0:
                part = jnp.where(lane[:8] < 2, first_product[8 * peer:8 * peer + 8], part)
            start = pad + 16 * peer + 8 * (tile // 2)
            rows_ref[start:start + 8, LANES * (tile % 2):LANES * (tile % 2 + 1)] = part
    left_ref[0:16, :] = jnp.zeros((16, 512), bf16)
    for back in range(2):
        left_ref[16:, 256 * back:256 * (back + 1)] = rows_ref[pad - 8 * back:pad - 8 * back + 512, :].astype(bf16)

    lower = lanes_of((LANES, LANES)) >= rows_of((LANES, LANES))
    toep_ref[0] = jnp.zeros((LANES, LANES), bf16)
    turned = jnp.zeros((LANES, LANES), f32)
    for step in range(STEPS):
        for e in range(2 * DEPTH * step, 2 * DEPTH * (step + 1)):
            before = turned
            row = jnp.broadcast_to(lag_ref[2 * e:2 * e + 1, :], (LANES, LANES))
            turned = pltpu.roll(row, 0, 1, stride=1, stride_axis=0)
            toep_ref[e + 1] = jnp.where(lower, turned, before).astype(bf16)
        if TAIL <= step < STEPS - 1:
            continue
        head = TAIL if step == STEPS - 1 else step
        offset = 8 * DEPTH * head
        lefts, parts = [], []
        for part in range(head, step + 1):
            gap = 8 * DEPTH * (part - head)
            count = 512 - offset - gap
            left = jnp.concatenate((left_ref[16:16 + count, :], left_ref[0:count, :]), axis=1)
            if gap:
                left = jnp.concatenate((jnp.zeros((gap, 256 * DEPTH), bf16), left), axis=0)
            lefts.append(left)
            for back in range(DEPTH):
                for half in range(2):
                    at = 1 + 2 * (DEPTH * part + back) - half
                    parts.append(jnp.concatenate((toep_ref[at], toep_ref[at + 1]), axis=1))
        right = jnp.concatenate(parts, axis=0)
        got = jnp.dot(jnp.concatenate(lefts, axis=1), right, preferred_element_type=f32)
        if step == 0:
            sum_ref[...] = got
        else:
            sum_ref[offset:, :] += got

        for peer in range(DEPTH // 2 * head, DEPTH // 2 * (step + 1)):
            group = slice(8 * peer, 8 * peer + 8)
            result = sum_ref[16 * peer:16 * peer + 16, :].astype(bf16)
            head = result[0:8, 0:LANES].astype(f32)
            done = aux_ref[3] * first_query[group] * (head + aux_ref[4] * first_product[group])
            out_ref[place_back(peer), :, 0:LANES] = jnp.where(lane[:8] < 2, done, head).astype(bf16)
            out_ref[place_back(peer), :, LANES:256] = result[0:8, LANES:]
            out_ref[place_back(peer), :, 256:512] = result[8:16]


def shards(stream_q, stream_k, stream_v, short_taps, filters, live_mask, skip_gain):
    taps_wide = jnp.transpose(short_taps, (0, 2, 1))
    message = pl.pallas_call(
        message_kernel,
        out_shape=jax.ShapeDtypeStruct((PEERS, TILES + 1, 8, LANES), bf16),
        in_specs=[HBM] * 5,
        out_specs=HBM,
        scratch_shapes=[
            pltpu.VMEM((256, LANES), bf16),
            pltpu.VMEM((256, LANES), bf16),
            pltpu.VMEM((256, BLOCK), bf16),
            pltpu.VMEM((256, BLOCK), bf16),
            pltpu.VMEM((3, 3, 256), f32),
            pltpu.VMEM((16, BLOCK), f32),
            pltpu.VMEM((256, 6 * LANES), f32),
            pltpu.VMEM((PEERS, TILES + 1, 8, LANES), bf16),
            pltpu.SemaphoreType.DMA((6,)),
            pltpu.SemaphoreType.DMA((STORES,)),
        ],
        name="message",
    )(stream_q, stream_k, stream_v, taps_wide, filters)
    arrived = lax.all_to_all(message, "seq", split_axis=0, concat_axis=0, tiled=True, axis_index_groups=[ORDER_OUT])

    query, skip, aux = pl.pallas_call(
        gate_kernel,
        out_shape=[jax.ShapeDtypeStruct((256, BLOCK), f32)] * 2 + [jax.ShapeDtypeStruct((5, OWN, LANES), f32)],
        in_specs=[VMEM] * 6,
        out_specs=[VMEM] * 3,
        scratch_shapes=[pltpu.VMEM((256, 16), f32)],
        compiler_params=pltpu.CompilerParams(vmem_limit_bytes=16 << 20),
        cost_estimate=pl.CostEstimate(flops=4000000, bytes_accessed=2 << 20, transcendentals=0),
        name="gate",
    )(stream_q, stream_k, stream_v, taps_wide, live_mask[None, :], skip_gain[None, :])

    convolved = pl.pallas_call(
        conv_kernel,
        out_shape=jax.ShapeDtypeStruct((PEERS, OWN, BLOCK), bf16),
        in_specs=[VMEM] * 2,
        out_specs=VMEM,
        scratch_shapes=[
            pltpu.VMEM((256, LANES), f32),
            pltpu.VMEM((129, LANES, LANES), bf16),
            pltpu.VMEM((512 + 8 * (DEPTH - 1), 256), f32),
            pltpu.VMEM((528, 512), bf16),
            pltpu.VMEM((512, 256), f32),
        ],
        compiler_params=pltpu.CompilerParams(vmem_limit_bytes=32 << 20),
        cost_estimate=pl.CostEstimate(flops=2300000000, bytes_accessed=1 << 20, transcendentals=0),
        name="conv",
    )(arrived, aux)
    back = lax.all_to_all(convolved, "seq", split_axis=0, concat_axis=0, tiled=True, axis_index_groups=[ORDER_BACK])
    return pl.pallas_call(
        final_kernel,
        out_shape=jax.ShapeDtypeStruct((256, BLOCK), bf16),
        in_specs=[VMEM] * 3,
        out_specs=HBM,
        scratch_shapes=[pltpu.VMEM((256, BLOCK), bf16), pltpu.SemaphoreType.DMA((4,))],
        compiler_params=pltpu.CompilerParams(vmem_limit_bytes=16 << 20),
        name="final",
    )(back, query, skip)


def solution(mesh):
    in_specs = (
        P("tp", "seq"),
        P("tp", "seq"),
        P("tp", "seq"),
        P(None, "tp", None),
        P("tp", "seq"),
        P("tp"),
        P("tp"),
    )
    return jax.shard_map(shards, mesh=mesh, in_specs=in_specs, out_specs=P("tp", "seq"), check_vma=False)
```

```python
import jax
import jax.numpy as jnp
from jax import lax
from jax.experimental import pallas as pl
from jax.experimental.pallas import tpu as pltpu
from jax.sharding import PartitionSpec as P

f32, bf16 = jnp.float32, jnp.bfloat16
PEERS = 32
OWN = 8
BLOCK = 512
LANES = 128
TILES = BLOCK // LANES
FIRST_BACK = 17
IN_TURN = [index for step in range(PEERS // 2) for index in (step, step + PEERS // 2)]
ORDER_OUT = [
    23, 26, 17, 11, 10, 28, 1, 5, 4, 7, 16, 9, 19, 30, 13, 22,
    0, 21, 29, 6, 12, 20, 14, 15, 3, 31, 2, 24, 25, 27, 18, 8,
]
ORDER_BACK = [FIRST_BACK] + [index for index in IN_TURN if index != FIRST_BACK]


def own_group(index):
    half = PEERS // 2
    turn = 2 * lax.rem(index, half) + index // half
    return jnp.where(index == FIRST_BACK, 0, jnp.where(turn < IN_TURN.index(FIRST_BACK), turn + 1, turn))


def place_there(group):
    return ORDER_OUT.index(ORDER_BACK[group])


def place_from(block):
    return ORDER_OUT.index(block)


def place_back(block):
    return ORDER_BACK.index(block)


VMEM = pl.BlockSpec(memory_space=pltpu.VMEM)
HBM = pl.BlockSpec(memory_space=pltpu.HBM)


def lanes_of(shape):
    return lax.broadcasted_iota(jnp.int32, shape, 1)


def rows_of(shape):
    return lax.broadcasted_iota(jnp.int32, shape, 0)


def features(signal, taps):
    return (
        taps[:, 0:1] * signal
        + taps[:, 1:2] * pltpu.roll(signal, 1, 1)
        + taps[:, 2:3] * pltpu.roll(signal, 2, 1)
    )


def columns_of(rows):
    spare = 16 - sum(row.shape[0] for row in rows)
    return jnp.transpose(jnp.concatenate(list(rows) + [jnp.zeros((spare, 256), f32)], axis=0))


def spread_rows(rows):
    count = sum(row.shape[0] for row in rows)
    values = jnp.concatenate(list(rows) + [jnp.zeros((8 - count, 256), f32)], axis=0)
    terms = []
    for _ in range(3):
        terms.append(values.astype(bf16).astype(f32))
        values = values - terms[-1]
    shape = (24, LANES * count)
    pick = (rows_of(shape) % 8 == lanes_of(shape) // LANES).astype(bf16)
    columns = jnp.transpose(jnp.concatenate(terms, axis=0)).astype(bf16)
    return jnp.dot(columns, pick, preferred_element_type=f32)


STORES = 8


def message_kernel(q_hbm, k_hbm, v_hbm, taps_hbm, filt_hbm, out_hbm, qf, ql, kk, vv, taps_ref, filt_ref, wide_ref, out_ref, sems, out_sems):
    loads = [
        pltpu.make_async_copy(taps_hbm, taps_ref, sems.at[0]),
        pltpu.make_async_copy(k_hbm, kk, sems.at[1]),
        pltpu.make_async_copy(v_hbm, vv, sems.at[2]),
        pltpu.make_async_copy(filt_hbm, filt_ref, sems.at[3]),
        pltpu.make_async_copy(q_hbm.at[:, 0:LANES], qf, sems.at[4]),
        pltpu.make_async_copy(q_hbm.at[:, BLOCK - LANES:], ql, sems.at[5]),
    ]
    for copy in loads:
        copy.start()
    loads[0].wait()
    wide_ref[...] = spread_rows((taps_ref[1], taps_ref[2]))
    for copy in loads[1:]:
        copy.wait()
    lane = lanes_of((16, LANES))
    small_row = rows_of((8, LANES))
    group_at = {place_there(group): group for group in range(PEERS)}
    chunks = list(dict.fromkeys(group_at[place] // 2 for place in range(PEERS)))
    stores = []
    for done, chunk in enumerate(chunks):
        rows = slice(16 * chunk, 16 * chunk + 16)
        key = kk[rows, :].astype(f32)
        value = vv[rows, :].astype(f32)

        def features(signal, first):
            taps = [
                jnp.concatenate([wide_ref[rows, LANES * at:LANES * (at + 1)]] * TILES, axis=1)
                for at in range(first, first + 3)
            ]
            return taps[0] * signal + taps[1] * pltpu.roll(signal, 1, 1) + taps[2] * pltpu.roll(signal, 2, 1)

        product = features(key, 0) * features(value, 3)

        def ends(first, last, place):
            return pltpu.roll(jnp.where(lane >= 64, last, first), place, 1)

        k_ends = ends(key[:, 0:LANES], key[:, BLOCK - LANES:], 2)
        v_ends = ends(value[:, 0:LANES], value[:, BLOCK - LANES:], 6)
        q_ends = ends(qf[rows, :].astype(f32), ql[rows, :].astype(f32), 10)
        wide = jnp.where(small_row < 2, filt_ref[chunk:chunk + 1, 0:LANES],
                         jnp.where(small_row < 4, filt_ref[chunk:chunk + 1, LANES:2 * LANES],
                                   jnp.where(small_row < 6, filt_ref[chunk:chunk + 1, 2 * LANES:3 * LANES],
                                             filt_ref[chunk:chunk + 1, 3 * LANES:4 * LANES])))
        lags = jnp.where(small_row % 2 == 1, wide, pltpu.roll(wide, 64, 1))
        lags = jnp.concatenate((lags, lags), axis=0)
        edge = jnp.where(lane < 4, k_ends, jnp.where(lane < 8, v_ends, jnp.where(lane < 12, q_ends, lags)))
        for half in range(2):
            place = place_there(2 * chunk + half)
            piece = slice(8 * half, 8 * half + 8)
            for tile in range(TILES):
                out_ref[place, tile] = product[piece, LANES * tile:LANES * (tile + 1)].astype(bf16)
            out_ref[place, TILES] = edge[piece].astype(bf16)
        full = {place_there(2 * chunk + half) for chunk in chunks[:done + 1] for half in range(2)}
        while len(stores) < STORES:
            span = slice(PEERS // STORES * len(stores), PEERS // STORES * (len(stores) + 1))
            if not full.issuperset(range(span.start, span.stop)):
                break
            stores.append(pltpu.make_async_copy(out_ref.at[span], out_hbm.at[span], out_sems.at[len(stores)]))
            stores[-1].start()
    assert len(stores) == STORES
    for copy in stores:
        copy.wait()


def gate_kernel(q_ref, k_ref, v_ref, taps_ref, live_ref, gain_ref, query_ref, skip_ref, aux_ref, table_ref):
    table_ref[...] = columns_of(
        (taps_ref[0], taps_ref[1], taps_ref[2], live_ref[...].astype(f32), gain_ref[...])
    )
    own = table_ref[pl.ds(pl.multiple_of(own_group(lax.axis_index("seq")) * OWN, OWN), OWN), :]
    kind = lanes_of((OWN, LANES)) // 4
    for tap in range(3):
        aux_ref[tap] = jnp.where(
            kind == 0, own[:, 3 + tap:4 + tap], jnp.where(kind == 1, own[:, 6 + tap:7 + tap], own[:, tap:tap + 1])
        )
    for place in range(2):
        aux_ref[3 + place] = jnp.broadcast_to(own[:, 9 + place:10 + place], (OWN, LANES))
    for chunk in range(PEERS // 2):
        rows = slice(16 * chunk, 16 * chunk + 16)
        taps = table_ref[rows, :]
        feat_query = features(q_ref[rows, :].astype(f32), taps[:, 0:3])
        feat_key = features(k_ref[rows, :].astype(f32), taps[:, 3:6])
        feat_value = features(v_ref[rows, :].astype(f32), taps[:, 6:9])
        product = (feat_key * feat_value).astype(bf16).astype(f32)
        finished = lanes_of((16, BLOCK)) < 2
        query_ref[rows, :] = jnp.where(finished, 1.0, taps[:, 9:10] * feat_query)
        skip_ref[rows, :] = jnp.where(finished, 0.0, taps[:, 10:11] * product)


def final_kernel(back_ref, query_ref, skip_ref, out_hbm, out_ref, sems):
    parts = sems.shape[0]
    copies = []
    for part in range(parts):
        groups = slice(PEERS // parts * part, PEERS // parts * (part + 1))
        rows = slice(OWN * groups.start, OWN * groups.stop)
        back = back_ref[groups].astype(f32).reshape(OWN * PEERS // parts, BLOCK)
        out_ref[rows, :] = (query_ref[rows, :] * (back + skip_ref[rows, :])).astype(bf16)
        copies.append(pltpu.make_async_copy(out_ref.at[rows], out_hbm.at[rows], sems.at[part]))
        copies[-1].start()
    for copy in copies:
        copy.wait()


DEPTH = 4
STEPS = 64 // DEPTH
TAIL = 12


def conv_kernel(msg_ref, aux_ref, out_ref, lag_ref, toep_ref, rows_ref, left_ref, sum_ref):
    lane = lanes_of((256, LANES))
    pad = 8 * (DEPTH - 1)
    edge = jnp.concatenate([msg_ref[place_from(block), TILES].astype(f32) for block in range(PEERS)], axis=0)
    lag_ref[...] = jnp.where(lane < 64, pltpu.roll(edge, 64, 1), pltpu.roll(edge, 255, 0))

    earlier = jnp.concatenate((jnp.zeros((8, LANES), f32), edge[:-8]), axis=0)
    joined = jnp.where(lane % 4 < 2, earlier, edge)

    def spread(index):
        return jnp.concatenate([aux_ref[index]] * PEERS, axis=0)

    feat = (
        spread(0) * joined
        + spread(1) * pltpu.roll(joined, 1, 1)
        + spread(2) * pltpu.roll(joined, 2, 1)
    )
    first_product = pltpu.roll(feat * pltpu.roll(feat, LANES - 4, 1), LANES - 2, 1)
    first_product = first_product.astype(bf16).astype(f32)
    first_query = pltpu.roll(feat, LANES - 10, 1)

    rows_ref[0:pad, :] = jnp.zeros((pad, 256), f32)
    for peer in range(PEERS):
        for tile in range(TILES):
            part = msg_ref[place_from(peer), tile].astype(f32)
            if tile == 0:
                part = jnp.where(lane[:8] < 2, first_product[8 * peer:8 * peer + 8], part)
            start = pad + 16 * peer + 8 * (tile // 2)
            rows_ref[start:start + 8, LANES * (tile % 2):LANES * (tile % 2 + 1)] = part
    for back in range(DEPTH):
        left_ref[:, 256 * back:256 * (back + 1)] = rows_ref[pad - 8 * back:pad - 8 * back + 512, :].astype(bf16)

    lower = lanes_of((LANES, LANES)) >= rows_of((LANES, LANES))
    toep_ref[0] = jnp.zeros((LANES, LANES), bf16)
    turned = jnp.zeros((LANES, LANES), f32)
    for step in range(STEPS):
        for e in range(2 * DEPTH * step, 2 * DEPTH * (step + 1)):
            before = turned
            row = jnp.broadcast_to(lag_ref[2 * e:2 * e + 1, :], (LANES, LANES))
            turned = pltpu.roll(row, 0, 1, stride=1, stride_axis=0)
            toep_ref[e + 1] = jnp.where(lower, turned, before).astype(bf16)
        if TAIL <= step < STEPS - 1:
            continue
        head = TAIL if step == STEPS - 1 else step
        offset = 8 * DEPTH * head
        lefts, parts = [], []
        for part in range(head, step + 1):
            gap = 8 * DEPTH * (part - head)
            left = left_ref[0:512 - offset - gap, :]
            if gap:
                left = jnp.concatenate((jnp.zeros((gap, 256 * DEPTH), bf16), left), axis=0)
            lefts.append(left)
            for back in range(DEPTH):
                for half in range(2):
                    at = 1 + 2 * (DEPTH * part + back) - half
                    parts.append(jnp.concatenate((toep_ref[at], toep_ref[at + 1]), axis=1))
        right = jnp.concatenate(parts, axis=0)
        got = jnp.dot(jnp.concatenate(lefts, axis=1), right, preferred_element_type=f32)
        if step == 0:
            sum_ref[...] = got
        else:
            sum_ref[offset:, :] += got

        for peer in range(DEPTH // 2 * head, DEPTH // 2 * (step + 1)):
            group = slice(8 * peer, 8 * peer + 8)
            result = sum_ref[16 * peer:16 * peer + 16, :].astype(bf16)
            head = result[0:8, 0:LANES].astype(f32)
            done = aux_ref[3] * first_query[group] * (head + aux_ref[4] * first_product[group])
            out_ref[place_back(peer), :, 0:LANES] = jnp.where(lane[:8] < 2, done, head).astype(bf16)
            out_ref[place_back(peer), :, LANES:256] = result[0:8, LANES:]
            out_ref[place_back(peer), :, 256:512] = result[8:16]


def shards(stream_q, stream_k, stream_v, short_taps, filters, live_mask, skip_gain):
    taps_wide = jnp.transpose(short_taps, (0, 2, 1))
    message = pl.pallas_call(
        message_kernel,
        out_shape=jax.ShapeDtypeStruct((PEERS, TILES + 1, 8, LANES), bf16),
        in_specs=[HBM] * 5,
        out_specs=HBM,
        scratch_shapes=[
            pltpu.VMEM((256, LANES), bf16),
            pltpu.VMEM((256, LANES), bf16),
            pltpu.VMEM((256, BLOCK), bf16),
            pltpu.VMEM((256, BLOCK), bf16),
            pltpu.VMEM((3, 3, 256), f32),
            pltpu.VMEM((16, BLOCK), f32),
            pltpu.VMEM((256, 6 * LANES), f32),
            pltpu.VMEM((PEERS, TILES + 1, 8, LANES), bf16),
            pltpu.SemaphoreType.DMA((6,)),
            pltpu.SemaphoreType.DMA((STORES,)),
        ],
        name="message",
    )(stream_q, stream_k, stream_v, taps_wide, filters)
    arrived = lax.all_to_all(message, "seq", split_axis=0, concat_axis=0, tiled=True, axis_index_groups=[ORDER_OUT])

    query, skip, aux = pl.pallas_call(
        gate_kernel,
        out_shape=[jax.ShapeDtypeStruct((256, BLOCK), f32)] * 2 + [jax.ShapeDtypeStruct((5, OWN, LANES), f32)],
        in_specs=[VMEM] * 6,
        out_specs=[VMEM] * 3,
        scratch_shapes=[pltpu.VMEM((256, 16), f32)],
        compiler_params=pltpu.CompilerParams(vmem_limit_bytes=16 << 20),
        cost_estimate=pl.CostEstimate(flops=4000000, bytes_accessed=2 << 20, transcendentals=0),
        name="gate",
    )(stream_q, stream_k, stream_v, taps_wide, live_mask[None, :], skip_gain[None, :])

    convolved = pl.pallas_call(
        conv_kernel,
        out_shape=jax.ShapeDtypeStruct((PEERS, OWN, BLOCK), bf16),
        in_specs=[VMEM] * 2,
        out_specs=VMEM,
        scratch_shapes=[
            pltpu.VMEM((256, LANES), f32),
            pltpu.VMEM((129, LANES, LANES), bf16),
            pltpu.VMEM((512 + 8 * (DEPTH - 1), 256), f32),
            pltpu.VMEM((512, 256 * DEPTH), bf16),
            pltpu.VMEM((512, 256), f32),
        ],
        compiler_params=pltpu.CompilerParams(vmem_limit_bytes=32 << 20),
        cost_estimate=pl.CostEstimate(flops=2300000000, bytes_accessed=1 << 20, transcendentals=0),
        name="conv",
    )(arrived, aux)
    back = lax.all_to_all(convolved, "seq", split_axis=0, concat_axis=0, tiled=True, axis_index_groups=[ORDER_BACK])
    return pl.pallas_call(
        final_kernel,
        out_shape=jax.ShapeDtypeStruct((256, BLOCK), bf16),
        in_specs=[VMEM] * 3,
        out_specs=HBM,
        scratch_shapes=[pltpu.VMEM((256, BLOCK), bf16), pltpu.SemaphoreType.DMA((4,))],
        compiler_params=pltpu.CompilerParams(vmem_limit_bytes=16 << 20),
        name="final",
    )(back, query, skip)


def solution(mesh):
    in_specs = (
        P("tp", "seq"),
        P("tp", "seq"),
        P("tp", "seq"),
        P(None, "tp", None),
        P("tp", "seq"),
        P("tp"),
        P("tp"),
    )
    return jax.shard_map(shards, mesh=mesh, in_specs=in_specs, out_specs=P("tp", "seq"), check_vma=False)
```

```python
import jax
import jax.numpy as jnp
from jax import lax
from jax.experimental import pallas as pl
from jax.experimental.pallas import tpu as pltpu
from jax.sharding import PartitionSpec as P

f32, bf16 = jnp.float32, jnp.bfloat16
PEERS = 32
OWN = 8
BLOCK = 512
LANES = 128
TILES = BLOCK // LANES
FIRST_BACK = 17
IN_TURN = [index for step in range(PEERS // 2) for index in (step, step + PEERS // 2)]
ORDER_OUT = [
    23, 26, 17, 11, 10, 28, 1, 5, 4, 7, 16, 9, 19, 30, 13, 22,
    0, 21, 29, 6, 12, 20, 14, 15, 3, 31, 2, 24, 25, 27, 18, 8,
]
ORDER_BACK = [FIRST_BACK] + [index for index in IN_TURN if index != FIRST_BACK]


def own_group(index):
    half = PEERS // 2
    turn = 2 * lax.rem(index, half) + index // half
    return jnp.where(index == FIRST_BACK, 0, jnp.where(turn < IN_TURN.index(FIRST_BACK), turn + 1, turn))


def place_there(group):
    return ORDER_OUT.index(ORDER_BACK[group])


def place_from(block):
    return ORDER_OUT.index(block)


def place_back(block):
    return ORDER_BACK.index(block)


VMEM = pl.BlockSpec(memory_space=pltpu.VMEM)
HBM = pl.BlockSpec(memory_space=pltpu.HBM)


def lanes_of(shape):
    return lax.broadcasted_iota(jnp.int32, shape, 1)


def rows_of(shape):
    return lax.broadcasted_iota(jnp.int32, shape, 0)


def features(signal, taps):
    return (
        taps[:, 0:1] * signal
        + taps[:, 1:2] * pltpu.roll(signal, 1, 1)
        + taps[:, 2:3] * pltpu.roll(signal, 2, 1)
    )


def columns_of(rows):
    spare = 16 - sum(row.shape[0] for row in rows)
    return jnp.transpose(jnp.concatenate(list(rows) + [jnp.zeros((spare, 256), f32)], axis=0))


def spread_rows(rows):
    count = sum(row.shape[0] for row in rows)
    values = jnp.concatenate(list(rows) + [jnp.zeros((8 - count, 256), f32)], axis=0)
    terms = []
    for _ in range(3):
        terms.append(values.astype(bf16).astype(f32))
        values = values - terms[-1]
    shape = (24, LANES * count)
    pick = (rows_of(shape) % 8 == lanes_of(shape) // LANES).astype(bf16)
    columns = jnp.transpose(jnp.concatenate(terms, axis=0)).astype(bf16)
    return jnp.dot(columns, pick, preferred_element_type=f32)


STORES = 4


def message_kernel(q_hbm, k_hbm, v_hbm, taps_hbm, filt_hbm, out_hbm, qf, ql, kk, vv, taps_ref, filt_ref, wide_ref, out_ref, sems, out_sems):
    loads = [
        pltpu.make_async_copy(taps_hbm, taps_ref, sems.at[0]),
        pltpu.make_async_copy(k_hbm, kk, sems.at[1]),
        pltpu.make_async_copy(v_hbm, vv, sems.at[2]),
        pltpu.make_async_copy(filt_hbm, filt_ref, sems.at[3]),
        pltpu.make_async_copy(q_hbm.at[:, 0:LANES], qf, sems.at[4]),
        pltpu.make_async_copy(q_hbm.at[:, BLOCK - LANES:], ql, sems.at[5]),
    ]
    for copy in loads:
        copy.start()
    loads[0].wait()
    wide_ref[...] = spread_rows((taps_ref[1], taps_ref[2]))
    for copy in loads[1:]:
        copy.wait()
    lane = lanes_of((16, LANES))
    small_row = rows_of((8, LANES))
    group_at = {place_there(group): group for group in range(PEERS)}
    chunks = list(dict.fromkeys(group_at[place] // 2 for place in range(PEERS)))
    stores = []
    for done, chunk in enumerate(chunks):
        rows = slice(16 * chunk, 16 * chunk + 16)
        key = kk[rows, :].astype(f32)
        value = vv[rows, :].astype(f32)

        def features(signal, first):
            taps = [
                jnp.concatenate([wide_ref[rows, LANES * at:LANES * (at + 1)]] * TILES, axis=1)
                for at in range(first, first + 3)
            ]
            return taps[0] * signal + taps[1] * pltpu.roll(signal, 1, 1) + taps[2] * pltpu.roll(signal, 2, 1)

        product = features(key, 0) * features(value, 3)

        def ends(first, last, place):
            return pltpu.roll(jnp.where(lane >= 64, last, first), place, 1)

        k_ends = ends(key[:, 0:LANES], key[:, BLOCK - LANES:], 2)
        v_ends = ends(value[:, 0:LANES], value[:, BLOCK - LANES:], 6)
        q_ends = ends(qf[rows, :].astype(f32), ql[rows, :].astype(f32), 10)
        wide = jnp.where(small_row < 2, filt_ref[chunk:chunk + 1, 0:LANES],
                         jnp.where(small_row < 4, filt_ref[chunk:chunk + 1, LANES:2 * LANES],
                                   jnp.where(small_row < 6, filt_ref[chunk:chunk + 1, 2 * LANES:3 * LANES],
                                             filt_ref[chunk:chunk + 1, 3 * LANES:4 * LANES])))
        lags = jnp.where(small_row % 2 == 1, wide, pltpu.roll(wide, 64, 1))
        lags = jnp.concatenate((lags, lags), axis=0)
        edge = jnp.where(lane < 4, k_ends, jnp.where(lane < 8, v_ends, jnp.where(lane < 12, q_ends, lags)))
        for half in range(2):
            place = place_there(2 * chunk + half)
            piece = slice(8 * half, 8 * half + 8)
            for tile in range(TILES):
                out_ref[place, tile] = product[piece, LANES * tile:LANES * (tile + 1)].astype(bf16)
            out_ref[place, TILES] = edge[piece].astype(bf16)
        full = {place_there(2 * chunk + half) for chunk in chunks[:done + 1] for half in range(2)}
        while len(stores) < STORES:
            span = slice(PEERS // STORES * len(stores), PEERS // STORES * (len(stores) + 1))
            if not full.issuperset(range(span.start, span.stop)):
                break
            stores.append(pltpu.make_async_copy(out_ref.at[span], out_hbm.at[span], out_sems.at[len(stores)]))
            stores[-1].start()
    assert len(stores) == STORES
    for copy in stores:
        copy.wait()


def gate_kernel(q_ref, k_ref, v_ref, taps_ref, live_ref, gain_ref, query_ref, skip_ref, aux_ref, table_ref):
    table_ref[...] = columns_of(
        (taps_ref[0], taps_ref[1], taps_ref[2], live_ref[...].astype(f32), gain_ref[...])
    )
    own = table_ref[pl.ds(pl.multiple_of(own_group(lax.axis_index("seq")) * OWN, OWN), OWN), :]
    kind = lanes_of((OWN, LANES)) // 4
    for tap in range(3):
        aux_ref[tap] = jnp.where(
            kind == 0, own[:, 3 + tap:4 + tap], jnp.where(kind == 1, own[:, 6 + tap:7 + tap], own[:, tap:tap + 1])
        )
    for place in range(2):
        aux_ref[3 + place] = jnp.broadcast_to(own[:, 9 + place:10 + place], (OWN, LANES))
    for chunk in range(PEERS // 2):
        rows = slice(16 * chunk, 16 * chunk + 16)
        taps = table_ref[rows, :]
        feat_query = features(q_ref[rows, :].astype(f32), taps[:, 0:3])
        feat_key = features(k_ref[rows, :].astype(f32), taps[:, 3:6])
        feat_value = features(v_ref[rows, :].astype(f32), taps[:, 6:9])
        product = (feat_key * feat_value).astype(bf16).astype(f32)
        finished = lanes_of((16, BLOCK)) < 2
        query_ref[rows, :] = jnp.where(finished, 1.0, taps[:, 9:10] * feat_query)
        skip_ref[rows, :] = jnp.where(finished, 0.0, taps[:, 10:11] * product)


def final_kernel(back_ref, query_ref, skip_ref, out_hbm, out_ref, sems):
    parts = sems.shape[0]
    copies = []
    for part in range(parts):
        groups = slice(PEERS // parts * part, PEERS // parts * (part + 1))
        rows = slice(OWN * groups.start, OWN * groups.stop)
        back = back_ref[groups].astype(f32).reshape(OWN * PEERS // parts, BLOCK)
        out_ref[rows, :] = (query_ref[rows, :] * (back + skip_ref[rows, :])).astype(bf16)
        copies.append(pltpu.make_async_copy(out_ref.at[rows], out_hbm.at[rows], sems.at[part]))
        copies[-1].start()
    for copy in copies:
        copy.wait()


DEPTH = 4
STEPS = 64 // DEPTH
TAIL = 12


def conv_kernel(msg_ref, aux_ref, out_ref, lag_ref, toep_ref, rows_ref, left_ref, sum_ref):
    lane = lanes_of((256, LANES))
    pad = 8 * (DEPTH - 1)
    edge = jnp.concatenate([msg_ref[place_from(block), TILES].astype(f32) for block in range(PEERS)], axis=0)
    lag_ref[...] = jnp.where(lane < 64, pltpu.roll(edge, 64, 1), pltpu.roll(edge, 255, 0))

    earlier = jnp.concatenate((jnp.zeros((8, LANES), f32), edge[:-8]), axis=0)
    joined = jnp.where(lane % 4 < 2, earlier, edge)

    def spread(index):
        return jnp.concatenate([aux_ref[index]] * PEERS, axis=0)

    feat = (
        spread(0) * joined
        + spread(1) * pltpu.roll(joined, 1, 1)
        + spread(2) * pltpu.roll(joined, 2, 1)
    )
    first_product = pltpu.roll(feat * pltpu.roll(feat, LANES - 4, 1), LANES - 2, 1)
    first_product = first_product.astype(bf16).astype(f32)
    first_query = pltpu.roll(feat, LANES - 10, 1)

    rows_ref[0:pad, :] = jnp.zeros((pad, 256), f32)
    for peer in range(PEERS):
        for tile in range(TILES):
            part = msg_ref[place_from(peer), tile].astype(f32)
            if tile == 0:
                part = jnp.where(lane[:8] < 2, first_product[8 * peer:8 * peer + 8], part)
            start = pad + 16 * peer + 8 * (tile // 2)
            rows_ref[start:start + 8, LANES * (tile % 2):LANES * (tile % 2 + 1)] = part
    for back in range(DEPTH):
        left_ref[:, 256 * back:256 * (back + 1)] = rows_ref[pad - 8 * back:pad - 8 * back + 512, :].astype(bf16)

    lower = lanes_of((LANES, LANES)) >= rows_of((LANES, LANES))
    toep_ref[0] = jnp.zeros((LANES, LANES), bf16)
    turned = jnp.zeros((LANES, LANES), f32)
    for step in range(STEPS):
        for e in range(2 * DEPTH * step, 2 * DEPTH * (step + 1)):
            before = turned
            row = jnp.broadcast_to(lag_ref[2 * e:2 * e + 1, :], (LANES, LANES))
            turned = pltpu.roll(row, 0, 1, stride=1, stride_axis=0)
            toep_ref[e + 1] = jnp.where(lower, turned, before).astype(bf16)
        if TAIL <= step < STEPS - 1:
            continue
        head = TAIL if step == STEPS - 1 else step
        offset = 8 * DEPTH * head
        lefts, parts = [], []
        for part in range(head, step + 1):
            gap = 8 * DEPTH * (part - head)
            left = left_ref[0:512 - offset - gap, :]
            if gap:
                left = jnp.concatenate((jnp.zeros((gap, 256 * DEPTH), bf16), left), axis=0)
            lefts.append(left)
            for back in range(DEPTH):
                for half in range(2):
                    at = 1 + 2 * (DEPTH * part + back) - half
                    parts.append(jnp.concatenate((toep_ref[at], toep_ref[at + 1]), axis=1))
        right = jnp.concatenate(parts, axis=0)
        got = jnp.dot(jnp.concatenate(lefts, axis=1), right, preferred_element_type=f32)
        if step == 0:
            sum_ref[...] = got
        else:
            sum_ref[offset:, :] += got

        for peer in range(DEPTH // 2 * head, DEPTH // 2 * (step + 1)):
            group = slice(8 * peer, 8 * peer + 8)
            result = sum_ref[16 * peer:16 * peer + 16, :].astype(bf16)
            head = result[0:8, 0:LANES].astype(f32)
            done = aux_ref[3] * first_query[group] * (head + aux_ref[4] * first_product[group])
            out_ref[place_back(peer), :, 0:LANES] = jnp.where(lane[:8] < 2, done, head).astype(bf16)
            out_ref[place_back(peer), :, LANES:256] = result[0:8, LANES:]
            out_ref[place_back(peer), :, 256:512] = result[8:16]


def shards(stream_q, stream_k, stream_v, short_taps, filters, live_mask, skip_gain):
    taps_wide = jnp.transpose(short_taps, (0, 2, 1))
    message = pl.pallas_call(
        message_kernel,
        out_shape=jax.ShapeDtypeStruct((PEERS, TILES + 1, 8, LANES), bf16),
        in_specs=[HBM] * 5,
        out_specs=HBM,
        scratch_shapes=[
            pltpu.VMEM((256, LANES), bf16),
            pltpu.VMEM((256, LANES), bf16),
            pltpu.VMEM((256, BLOCK), bf16),
            pltpu.VMEM((256, BLOCK), bf16),
            pltpu.VMEM((3, 3, 256), f32),
            pltpu.VMEM((16, BLOCK), f32),
            pltpu.VMEM((256, 6 * LANES), f32),
            pltpu.VMEM((PEERS, TILES + 1, 8, LANES), bf16),
            pltpu.SemaphoreType.DMA((6,)),
            pltpu.SemaphoreType.DMA((STORES,)),
        ],
        name="message",
    )(stream_q, stream_k, stream_v, taps_wide, filters)
    arrived = lax.all_to_all(message, "seq", split_axis=0, concat_axis=0, tiled=True, axis_index_groups=[ORDER_OUT])

    query, skip, aux = pl.pallas_call(
        gate_kernel,
        out_shape=[jax.ShapeDtypeStruct((256, BLOCK), f32)] * 2 + [jax.ShapeDtypeStruct((5, OWN, LANES), f32)],
        in_specs=[VMEM] * 6,
        out_specs=[VMEM] * 3,
        scratch_shapes=[pltpu.VMEM((256, 16), f32)],
        compiler_params=pltpu.CompilerParams(vmem_limit_bytes=16 << 20),
        cost_estimate=pl.CostEstimate(flops=4000000, bytes_accessed=2 << 20, transcendentals=0),
        name="gate",
    )(stream_q, stream_k, stream_v, taps_wide, live_mask[None, :], skip_gain[None, :])

    convolved = pl.pallas_call(
        conv_kernel,
        out_shape=jax.ShapeDtypeStruct((PEERS, OWN, BLOCK), bf16),
        in_specs=[VMEM] * 2,
        out_specs=VMEM,
        scratch_shapes=[
            pltpu.VMEM((256, LANES), f32),
            pltpu.VMEM((129, LANES, LANES), bf16),
            pltpu.VMEM((512 + 8 * (DEPTH - 1), 256), f32),
            pltpu.VMEM((512, 256 * DEPTH), bf16),
            pltpu.VMEM((512, 256), f32),
        ],
        compiler_params=pltpu.CompilerParams(vmem_limit_bytes=32 << 20),
        cost_estimate=pl.CostEstimate(flops=2300000000, bytes_accessed=1 << 20, transcendentals=0),
        name="conv",
    )(arrived, aux)
    back = lax.all_to_all(convolved, "seq", split_axis=0, concat_axis=0, tiled=True, axis_index_groups=[ORDER_BACK])
    return pl.pallas_call(
        final_kernel,
        out_shape=jax.ShapeDtypeStruct((256, BLOCK), bf16),
        in_specs=[VMEM] * 3,
        out_specs=HBM,
        scratch_shapes=[pltpu.VMEM((256, BLOCK), bf16), pltpu.SemaphoreType.DMA((2,))],
        compiler_params=pltpu.CompilerParams(vmem_limit_bytes=16 << 20),
        name="final",
    )(back, query, skip)


def solution(mesh):
    in_specs = (
        P("tp", "seq"),
        P("tp", "seq"),
        P("tp", "seq"),
        P(None, "tp", None),
        P("tp", "seq"),
        P("tp"),
        P("tp"),
    )
    return jax.shard_map(shards, mesh=mesh, in_specs=in_specs, out_specs=P("tp", "seq"), check_vma=False)
```
